512 devices in a mesh: dp: 512 (over y, x, z, core).
Axes of the slice: x: 4, y: 8, z: 8, core: 2. Of those that a mesh axis runs over, the one named last changes fastest.
Arguments:
- image_feats: bfloat16 [131072, 1152], P('dp'), may hold values from -180 to 180
- text_embeds: bfloat16 [131072, 640], P('dp'), may hold values from -180 to 180
- head_weight: bfloat16 [1152, 640], replicated, may hold values from -0.1875 to 0.1875
- logit_scale: float32 [1], replicated, may hold values from 5 to 15
- logit_bias: float32 [1], replicated, may hold values from -6 to -2
Outputs:
- loss: float32 [], replicated
- image_grad: bfloat16 [131072, 1152], P('dp')
- text_grad: bfloat16 [131072, 640], P('dp')
- head_grad: bfloat16 [1152, 640], replicated
The draws below stay inside these ranges and needn't reach their ends.
All inputs are finite; a program needn't handle non-finite values.
Results may differ from the reference program's by a relative error of at most 0.0064.
Values may be sent and summed in bfloat16 or wider, within the bound.
No kernel may reach another device: no remote copies, remote signals or barrier semaphores. Data moves between devices by JAX's collectives and lax.ppermute only.
A program may use at most 64 MiB of HBM per device.

```python
import math
import jax
import jax.numpy as jnp
from jax import lax

D = 1152
E = 640
TOK_DEV = 256
HOPS = 4
TOKENS = 131072


def scaled_rows(key, base, rows, cols):
    key_a, key_b = jax.random.split(key)
    row_scale = jnp.exp(jax.random.uniform(key_a, (rows, 1), jnp.float32, 0.0, math.log(10.0)))
    col_scale = jnp.exp(jax.random.uniform(key_b, (1, cols), jnp.float32, 0.0, math.log(10.0)))
    return (jnp.clip(base, -6.0, 6.0) * row_scale * col_scale * 0.3).astype(jnp.bfloat16)


def draw_image_feats(key, part):
    key = jax.random.fold_in(key, 11)
    key_s, key_c = jax.random.split(key, 2)
    base = jax.random.normal(key_c, (TOKENS, D), jnp.float32)
    return scaled_rows(key_s, base, TOKENS, D)


def draw_text_embeds(key, part):
    key = jax.random.fold_in(key, 23)
    key_s, key_c = jax.random.split(key, 2)
    base = jax.random.normal(key_c, (TOKENS, E), jnp.float32)
    return scaled_rows(key_s, base, TOKENS, E)


def normal_values(own_key, extent, spread, reach, kind=jnp.bfloat16):
    result = spread * jax.random.normal(own_key, extent, jnp.float32)
    return jnp.clip(result, min=-reach, max=reach).astype(kind)


def setup_inputs(seed: int = 0) -> dict:
    key_of = jax.random.split(jax.random.key(seed), 6)
    return {
        "image_feats": draw_image_feats(jax.random.fold_in(key_of[5], 71), 0),
        "text_embeds": draw_text_embeds(jax.random.fold_in(key_of[5], 71), 0),
        "head_weight": normal_values(key_of[2], (D, E), D ** -0.5, 0.1875),
        "logit_scale": jnp.clip(jnp.exp(jax.random.uniform(key_of[3], (1,), jnp.float32, math.log(5.0), math.log(15.0))), 5.0, 15.0),
        "logit_bias": jnp.clip(jax.random.uniform(key_of[4], (1,), jnp.float32, -6.0, -2.0), -6.0, -2.0),
    }


EPS = 1e-06

def reference(image_feats, text_embeds, head_weight, logit_scale, logit_bias):
    scale = logit_scale[0]
    bias = logit_bias[0]
    blocks = TOKENS // TOK_DEV
    u_full = jnp.dot(image_feats, head_weight, preferred_element_type=jnp.float32)
    inv_u = lax.rsqrt(lax.optimization_barrier(jnp.sum(u_full * u_full, axis=1, keepdims=True)) + EPS)
    zi = u_full * inv_u
    zi_b = zi.astype(jnp.bfloat16)
    text_f = text_embeds.astype(jnp.float32)
    inv_y = lax.rsqrt(lax.optimization_barrier(jnp.sum(text_f * text_f, axis=1, keepdims=True)) + EPS)
    zt = text_f * inv_y
    zt_b = zt.astype(jnp.bfloat16)
    img_blocks = zi_b.reshape(blocks, TOK_DEV, E).astype(jnp.float32)
    txt_blocks = zt_b.reshape(blocks, TOK_DEV, E).astype(jnp.float32)
    loss_sum = jnp.zeros((), jnp.float32)
    dzi = jnp.zeros((blocks, TOK_DEV, E), jnp.float32)
    dzt = jnp.zeros((blocks, TOK_DEV, E), jnp.float32)
    for offset in range(-HOPS, HOPS + 1):
        rolled = jnp.roll(txt_blocks, -offset, axis=0)
        prods = jnp.einsum('nae,nce->nac', img_blocks, rolled)
        logits = scale * prods + bias
        if offset == 0:
            label = jnp.where(jnp.eye(TOK_DEV, dtype=bool), 1.0, -1.0).astype(jnp.float32)
        else:
            label = -jnp.ones((TOK_DEV, TOK_DEV), jnp.float32)
        loss_sum = loss_sum + jnp.sum(jax.nn.softplus(-label * logits))
        coef = (-label * jax.nn.sigmoid(-label * logits)).astype(jnp.bfloat16).astype(jnp.float32)
        dzi = dzi + scale * jnp.einsum('nac,nce->nae', coef, rolled)
        part = scale * jnp.einsum('nac,nae->nce', coef, img_blocks)
        dzt = dzt + jnp.roll(part, offset, axis=0)
    dzi = dzi.reshape(TOKENS, E)
    dzt = dzt.reshape(TOKENS, E)
    du = ((dzi - zi * lax.optimization_barrier(jnp.sum(zi * dzi, axis=1, keepdims=True))) * inv_u).astype(jnp.bfloat16)
    image_grad = jnp.dot(du, head_weight.T, preferred_element_type=jnp.float32).astype(jnp.bfloat16)
    head_total = jnp.dot(image_feats.T, du, preferred_element_type=jnp.float32)
    head_grad = (head_total / TOK_DEV).astype(jnp.bfloat16)
    text_grad = ((dzt - zt * lax.optimization_barrier(jnp.sum(zt * dzt, axis=1, keepdims=True))) * inv_y).astype(jnp.bfloat16)
    loss = loss_sum / TOKENS
    return (loss, image_grad, text_grad, head_grad)
```

```python
import functools

import jax
import jax.numpy as jnp
from jax import lax
from jax.experimental import pallas as pl
from jax.experimental.pallas import tpu as pltpu
from jax.sharding import Mesh, PartitionSpec as P

D = 1152
E = 640
ROWS = 256
HALF = D // 2
LANES = 128
EPS = 1e-06
CHUNK = 64

BF = jnp.bfloat16
F32 = jnp.float32
VMEM = pl.BlockSpec(memory_space=pltpu.VMEM)
SMEM = pl.BlockSpec(memory_space=pltpu.SMEM)
PARAMS = pltpu.CompilerParams(vmem_limit_bytes=32 * 1024 * 1024)


def call(body, out_shape, n_smem, n_vmem, out_specs, scratch=(), flops=0, bytes_accessed=0):
    return pl.pallas_call(
        body,
        out_shape=out_shape,
        in_specs=[SMEM] * n_smem + [VMEM] * n_vmem,
        out_specs=out_specs,
        scratch_shapes=list(scratch),
        compiler_params=PARAMS,
        cost_estimate=pl.CostEstimate(flops=flops, bytes_accessed=bytes_accessed, transcendentals=0),
    )


def project_kernel(core_ref, own_ref, other_ref, weight_ref, zi_ref, zib_ref, inv_ref, xt_ref, all_ref):
    for part, ref in enumerate((own_ref, other_ref)):
        rows = pl.ds(part * ROWS, ROWS)
        all_ref[:, part * ROWS : (part + 1) * ROWS] = ref[...].T
        u = jnp.dot(ref[...], weight_ref[...], preferred_element_type=F32)
        inv = lax.rsqrt(jnp.sum(u * u, axis=1, keepdims=True) + EPS)
        zi = u * inv
        zi_ref[rows, :] = zi
        zib_ref[rows, :] = zi.astype(BF)
        inv_ref[rows, :] = jnp.broadcast_to(inv, (ROWS, LANES))
    xt_ref[...] = all_ref[pl.ds(pl.multiple_of(core_ref[0] * HALF, HALF), HALF), :]


def score_kernel(parts, has_dzi, scal_ref, zib_ref, text_ref, *refs):
    dzi_in = None
    if has_dzi:
        dzi_in, *refs = refs
    dzi_ref, dzt_ref, loss_ref, s_ref, c_ref = refs
    scale = scal_ref[0]
    bias = scal_ref[1]
    loss = jnp.zeros((8, ROWS), F32)
    for order, (q, n, diag) in enumerate(parts):
        cols = pl.ds(q * ROWS, ROWS)
        text = text_ref[cols, :].astype(F32)
        inv = lax.rsqrt(jnp.sum(text * text, axis=1, keepdims=True) + EPS)
        ztb = (text * inv).astype(BF)
        zib = zib_ref[0:n, :]
        s_ref[0:n, :] = lax.dot_general(zib, ztb, (((1,), (1,)), ((), ())), preferred_element_type=F32)
        for start in range(0, n, CHUNK):
            v = scale * s_ref[start : start + CHUNK, :] + bias
            paired = diag and start < ROWS
            if paired:
                row = lax.broadcasted_iota(jnp.int32, (CHUNK, ROWS), 0) + start
                col = lax.broadcasted_iota(jnp.int32, (CHUNK, ROWS), 1)
                own = row == col
                v = jnp.where(own, -v, v)
            e = jnp.exp(v)
            w = 1.0 + e
            r = 1.0 / w
            c = e * r
            if paired:
                c = jnp.where(own, -c, c)
            c_ref[start : start + CHUNK, :] = c.astype(BF)
            lost = (e - (w - 1.0)) * r
            loss = loss + jnp.sum(lost.reshape(CHUNK // 8, 8, ROWS), axis=0)
            k = CHUNK // 4
            prod = (w[0:k] * w[k : 2 * k]) * (w[2 * k : 3 * k] * w[3 * k :])
            loss = loss + jnp.sum(jnp.log(prod).reshape(k // 8, 8, ROWS), axis=0)
        coef = c_ref[0:n, :]
        dzi = scale * jnp.dot(coef, ztb, preferred_element_type=F32)
        if order:
            dzi_ref[0:n, :] += dzi
        elif has_dzi:
            dzi_ref[...] = dzi_in[...] + dzi
        else:
            dzi_ref[...] = dzi
        dzt = scale * lax.dot_general(coef, zib, (((0,), (0,)), ((), ())), preferred_element_type=F32)
        dzt_ref[cols, :] = dzt.astype(dzt_ref.dtype)
    loss_ref[...] = loss


def score(parts, scal, zib, text, dzi, dzt_dtype):
    n = len(parts) * ROWS
    args = (scal, zib, text) + (() if dzi is None else (dzi,))
    return call(
        functools.partial(score_kernel, parts, dzi is not None),
        (
            jax.ShapeDtypeStruct((2 * ROWS, E), F32),
            jax.ShapeDtypeStruct((n, E), dzt_dtype),
            jax.ShapeDtypeStruct((8, ROWS), F32),
        ),
        1,
        len(args) - 1,
        (VMEM, VMEM, VMEM),
        scratch=(pltpu.VMEM((2 * ROWS, ROWS), F32), pltpu.VMEM((2 * ROWS, ROWS), BF)),
        flops=sum(6 * n * ROWS * E for _, n, _ in parts),
        bytes_accessed=4 << 20,
    )(*args)


def head_kernel(dzi_ref, sent_ref, zi_ref, inv_ref, xt_ref, la_ref, lb_ref, lc_ref, du_ref, flat_ref, all_ref):
    for part in range(2):
        rows = pl.ds(part * ROWS, ROWS)
        swapped = pl.ds((1 - part) * ROWS, ROWS)
        dzi = dzi_ref[rows, :] + sent_ref[swapped, :]
        zi = zi_ref[rows, :]
        along = jnp.sum(zi * dzi, axis=1, keepdims=True)
        du = ((dzi - zi * along) * inv_ref[rows, 0:1]).astype(BF)
        all_ref[rows, :] = du
        if part == 0:
            du_ref[...] = du
    for slab in range(E // LANES):
        part = jnp.dot(xt_ref[...], all_ref[:, slab * LANES : (slab + 1) * LANES], preferred_element_type=F32)
        flat_ref[slab * HALF : (slab + 1) * HALF, :] = part.astype(BF)
    loss = jnp.sum(la_ref[...] + lb_ref[...] + lc_ref[...])
    total = jnp.full((16, LANES), loss, F32)
    high = total.astype(BF).astype(F32)
    low = (total - high).astype(BF).astype(F32)
    row = lax.broadcasted_iota(jnp.int32, (16, LANES), 0)
    lane = lax.broadcasted_iota(jnp.int32, (16, LANES), 1)
    both = jnp.where(lane == 0, high, jnp.where(lane == 1, low, 0.0))
    base = (E // LANES) * HALF
    flat_ref[base : base + 16, :] = jnp.where(row == 0, both, 0.0).astype(BF)
    flat_ref[base + 16 :, :] = jnp.zeros((flat_ref.shape[0] - base - 16, LANES), BF)


def reduce_kernel(share, chip_ref, pieces_ref, out_ref, sum_ref):
    group = 4 * share
    groups = pieces_ref.shape[0] // group
    total = jnp.zeros((group, LANES), F32)
    for g in range(groups):
        total = total + pieces_ref[g * group : (g + 1) * group, :].astype(F32)
    sum_ref[...] = total
    total = sum_ref[0:share, :] + sum_ref[share : 2 * share, :]
    total = total + (sum_ref[2 * share : 3 * share, :] + sum_ref[3 * share :, :])
    total = total * (1.0 / ROWS)
    loss_row = (E // LANES) * HALF
    row = lax.broadcasted_iota(jnp.int32, (share, LANES), 0)
    lane = lax.broadcasted_iota(jnp.int32, (share, LANES), 1)
    is_loss = (row == loss_row % share) & (chip_ref[0] == loss_row // share)
    loss = jnp.sum(jnp.where(row == loss_row % share, total, 0.0), axis=(0, 1), keepdims=True)
    loss = jnp.broadcast_to(loss, (share, LANES))
    high = loss.astype(BF).astype(F32)
    terms = jnp.where(lane == 0, high, jnp.where(lane == 1, loss - high, 0.0))
    total = jnp.where(is_loss, terms, total)
    for k in range(4):
        sum_ref[k * share : (k + 1) * share, :] = total
    tile = sum_ref[...].astype(BF)
    for g in range(groups):
        out_ref[g * group : (g + 1) * group, :] = tile


def assemble_kernel(core_ref, own_ref, other_ref, head_ref, loss_ref):
    core = core_ref[0]
    for slab in range(E // LANES):
        for ref, half in ((own_ref, core), (other_ref, 1 - core)):
            rows = pl.ds(pl.multiple_of(half * HALF, HALF), HALF)
            head_ref[rows, slab * LANES : (slab + 1) * LANES] = ref[slab * HALF : (slab + 1) * HALF, :]
    base = (E // LANES) * HALF
    terms = own_ref[base : base + 16, :].astype(F32) + other_ref[base : base + 16, :].astype(F32)
    loss_ref[0, 0] = jnp.sum(terms)


def text_kernel(own_ref, far_ref, near_ref, text_ref, out_ref):
    dzt = own_ref[...] + far_ref[0:ROWS, :].astype(F32) + near_ref[...].astype(F32)
    text = text_ref[...].astype(F32)
    inv = lax.rsqrt(jnp.sum(text * text, axis=1, keepdims=True) + EPS)
    zt = text * inv
    along = jnp.sum(zt * dzt, axis=1, keepdims=True)
    out_ref[...] = ((dzt - zt * along) * inv).astype(BF)


def per_device(chips, image_feats, text_embeds, head_weight, logit_scale, logit_bias):
    axes = ("chip", "core")
    core = lax.axis_index("core")
    core_id = core.astype(jnp.int32).reshape(1)
    chip_id = lax.axis_index("chip").astype(jnp.int32).reshape(1)
    across = [(i, i ^ 1) for i in range(2 * chips)]
    onward = [(2 * k + b, 2 * ((k + 1 - 2 * b) % chips) + b) for k in range(chips) for b in range(2)]
    back = [(d, s) for s, d in onward]
    scal = jnp.concatenate([logit_scale, logit_bias])

    text_other = lax.ppermute(text_embeds, axes, across)
    x_other = lax.ppermute(image_feats, axes, across)
    texts0 = jnp.concatenate([text_embeds, text_other])
    texts1 = lax.ppermute(texts0, axes, onward)
    texts2 = lax.ppermute(texts1, axes, onward)

    zi, zib, inv_u, x_half = call(
        project_kernel,
        (
            jax.ShapeDtypeStruct((2 * ROWS, E), F32),
            jax.ShapeDtypeStruct((2 * ROWS, E), BF),
            jax.ShapeDtypeStruct((2 * ROWS, LANES), F32),
            jax.ShapeDtypeStruct((HALF, 2 * ROWS), BF),
        ),
        1,
        3,
        (VMEM, VMEM, VMEM, VMEM),
        scratch=(pltpu.VMEM((D, 2 * ROWS), BF),),
        flops=2 * 2 * ROWS * D * E,
        bytes_accessed=5 << 20,
    )(core_id, image_feats, x_other, head_weight)

    both = 2 * ROWS
    dzi, dzt0, loss0 = score([(0, both, True)], scal, zib, text_embeds, None, F32)
    dzi, dzt1, loss1 = score([(0, both, False), (1, both, False)], scal, zib, texts1, dzi, F32)
    dzi, dzt2, loss2 = score([(1, both, False), (0, ROWS, False)], scal, zib, texts2, dzi, BF)
    dzi_sent = lax.ppermute(dzi, axes, across)
    far = lax.ppermute(dzt2, axes, back)

    flat_rows = 3072
    du, flat = call(
        head_kernel,
        (
            jax.ShapeDtypeStruct((ROWS, E), BF),
            jax.ShapeDtypeStruct((flat_rows, LANES), BF),
        ),
        0,
        8,
        (VMEM, VMEM),
        scratch=(pltpu.VMEM((2 * ROWS, E), BF),),
        flops=2 * 2 * ROWS * HALF * E,
        bytes_accessed=7 << 20,
    )(dzi, dzi_sent, zi, inv_u, x_half, loss0, loss1, loss2)

    dzt1, _ = lax.optimization_barrier((dzt1, flat))
    near = (far.astype(F32) + dzt1).astype(BF)
    near = lax.ppermute(near, axes, back)

    share = flat_rows // chips
    pieces = lax.all_to_all(flat.reshape(chips, share // 2, 2, LANES), "chip", 0, 0)
    spread = call(
        functools.partial(reduce_kernel, share),
        jax.ShapeDtypeStruct((flat_rows, LANES), BF),
        1,
        1,
        VMEM,
        scratch=(pltpu.VMEM((4 * share, LANES), F32),),
        flops=flat_rows * LANES,
        bytes_accessed=2 << 20,
    )(chip_id, pieces.reshape(flat_rows, LANES)).reshape(chips, share // 2, 2, LANES)
    half = lax.all_to_all(spread, "chip", 0, 0).reshape(flat_rows, LANES)
    half_other = lax.ppermute(half, axes, across)

    near_other = lax.ppermute(near[ROWS:], axes, across)
    image_grad = lax.dot_general(du, head_weight, (((1,), (1,)), ((), ())), preferred_element_type=F32).astype(BF)
    text_grad = call(
        text_kernel, jax.ShapeDtypeStruct((ROWS, E), BF), 0, 4, VMEM, flops=10 * ROWS * E, bytes_accessed=3 << 20
    )(dzt0, near, near_other, text_embeds)

    head_grad, loss = call(
        assemble_kernel,
        (jax.ShapeDtypeStruct((D, E), BF), jax.ShapeDtypeStruct((1, 1), F32)),
        1,
        2,
        (VMEM, SMEM),
        flops=1,
        bytes_accessed=3 << 20,
    )(core_id, half, half_other)
    loss = loss[0, 0] / (2 * chips)
    return (loss, image_grad, text_grad, head_grad)


def solution(mesh):
    chips = mesh.devices.size // 2
    by_chip = Mesh(mesh.devices.reshape(chips, 2), ("chip", "core"))
    rows = P(("chip", "core"), None)
    return jax.shard_map(
        functools.partial(per_device, chips),
        mesh=by_chip,
        in_specs=(rows, rows, P(), P(), P()),
        out_specs=(P(), rows, rows, P()),
        check_vma=False,
    )
```

```python
import functools

import jax
import jax.numpy as jnp
from jax import lax
from jax.experimental import pallas as pl
from jax.experimental.pallas import tpu as pltpu
from jax.sharding import Mesh, PartitionSpec as P

D = 1152
E = 640
ROWS = 256
HALF = D // 2
LANES = 128
EPS = 1e-06
CHUNK = 64

BF = jnp.bfloat16
F32 = jnp.float32
VMEM = pl.BlockSpec(memory_space=pltpu.VMEM)
SMEM = pl.BlockSpec(memory_space=pltpu.SMEM)
PARAMS = pltpu.CompilerParams(vmem_limit_bytes=10 * 1024 * 1024)


def call(body, out_shape, n_smem, n_vmem, out_specs, scratch=(), flops=0, bytes_accessed=0):
    return pl.pallas_call(
        body,
        out_shape=out_shape,
        in_specs=[SMEM] * n_smem + [VMEM] * n_vmem,
        out_specs=out_specs,
        scratch_shapes=list(scratch),
        compiler_params=PARAMS,
        cost_estimate=pl.CostEstimate(flops=flops, bytes_accessed=bytes_accessed, transcendentals=0),
    )


def project_kernel(core_ref, own_ref, other_ref, weight_ref, zi_ref, zib_ref, inv_ref, xt_ref, all_ref):
    for part, ref in enumerate((own_ref, other_ref)):
        rows = pl.ds(part * ROWS, ROWS)
        all_ref[:, part * ROWS : (part + 1) * ROWS] = ref[...].T
        u = jnp.dot(ref[...], weight_ref[...], preferred_element_type=F32)
        inv = lax.rsqrt(jnp.sum(u * u, axis=1, keepdims=True) + EPS)
        zi = u * inv
        zi_ref[rows, :] = zi
        zib_ref[rows, :] = zi.astype(BF)
        inv_ref[rows, :] = jnp.broadcast_to(inv, (ROWS, LANES))
    xt_ref[...] = all_ref[pl.ds(pl.multiple_of(core_ref[0] * HALF, HALF), HALF), :]


def score_kernel(parts, has_dzi, scal_ref, zib_ref, text_ref, *refs):
    dzi_in = None
    if has_dzi:
        dzi_in, *refs = refs
    dzi_ref, dzt_ref, loss_ref, s_ref, c_ref = refs
    scale = scal_ref[0]
    bias = scal_ref[1]
    loss = jnp.zeros((8, ROWS), F32)
    for order, (q, n, diag) in enumerate(parts):
        cols = pl.ds(q * ROWS, ROWS)
        text = text_ref[cols, :].astype(F32)
        inv = lax.rsqrt(jnp.sum(text * text, axis=1, keepdims=True) + EPS)
        ztb = (text * inv).astype(BF)
        zib = zib_ref[0:n, :]
        s_ref[0:n, :] = lax.dot_general(zib, ztb, (((1,), (1,)), ((), ())), preferred_element_type=F32)
        for start in range(0, n, CHUNK):
            v = scale * s_ref[start : start + CHUNK, :] + bias
            paired = diag and start < ROWS
            if paired:
                row = lax.broadcasted_iota(jnp.int32, (CHUNK, ROWS), 0) + start
                col = lax.broadcasted_iota(jnp.int32, (CHUNK, ROWS), 1)
                own = row == col
                v = jnp.where(own, -v, v)
            e = jnp.exp(v)
            w = 1.0 + e
            r = 1.0 / w
            c = e * r
            if paired:
                c = jnp.where(own, -c, c)
            c_ref[start : start + CHUNK, :] = c.astype(BF)
            lost = (e - (w - 1.0)) * r
            loss = loss + jnp.sum(lost.reshape(CHUNK // 8, 8, ROWS), axis=0)
            k = CHUNK // 4
            prod = (w[0:k] * w[k : 2 * k]) * (w[2 * k : 3 * k] * w[3 * k :])
            loss = loss + jnp.sum(jnp.log(prod).reshape(k // 8, 8, ROWS), axis=0)
        coef = c_ref[0:n, :]
        dzi = scale * jnp.dot(coef, ztb, preferred_element_type=F32)
        if order:
            dzi_ref[0:n, :] += dzi
        elif has_dzi:
            dzi_ref[...] = dzi_in[...] + dzi
        else:
            dzi_ref[...] = dzi
        dzt = scale * lax.dot_general(coef, zib, (((0,), (0,)), ((), ())), preferred_element_type=F32)
        dzt_ref[cols, :] = dzt.astype(dzt_ref.dtype)
    loss_ref[...] = loss


def score(parts, scal, zib, text, dzi, dzt_dtype):
    n = len(parts) * ROWS
    args = (scal, zib, text) + (() if dzi is None else (dzi,))
    return call(
        functools.partial(score_kernel, parts, dzi is not None),
        (
            jax.ShapeDtypeStruct((2 * ROWS, E), F32),
            jax.ShapeDtypeStruct((n, E), dzt_dtype),
            jax.ShapeDtypeStruct((8, ROWS), F32),
        ),
        1,
        len(args) - 1,
        (VMEM, VMEM, VMEM),
        scratch=(pltpu.VMEM((2 * ROWS, ROWS), F32), pltpu.VMEM((2 * ROWS, ROWS), BF)),
        flops=sum(6 * n * ROWS * E for _, n, _ in parts),
        bytes_accessed=4 << 20,
    )(*args)


def head_kernel(dzi_ref, sent_ref, zi_ref, inv_ref, xt_ref, la_ref, lb_ref, lc_ref, du_ref, flat_ref, all_ref):
    for part in range(2):
        rows = pl.ds(part * ROWS, ROWS)
        swapped = pl.ds((1 - part) * ROWS, ROWS)
        dzi = dzi_ref[rows, :] + sent_ref[swapped, :]
        zi = zi_ref[rows, :]
        along = jnp.sum(zi * dzi, axis=1, keepdims=True)
        du = ((dzi - zi * along) * inv_ref[rows, 0:1]).astype(BF)
        all_ref[rows, :] = du
        if part == 0:
            du_ref[...] = du
    for slab in range(E // LANES):
        part = jnp.dot(xt_ref[...], all_ref[:, slab * LANES : (slab + 1) * LANES], preferred_element_type=F32)
        flat_ref[slab * HALF : (slab + 1) * HALF, :] = part.astype(BF)
    loss = jnp.sum(la_ref[...] + lb_ref[...] + lc_ref[...])
    total = jnp.full((16, LANES), loss, F32)
    high = total.astype(BF).astype(F32)
    low = (total - high).astype(BF).astype(F32)
    row = lax.broadcasted_iota(jnp.int32, (16, LANES), 0)
    lane = lax.broadcasted_iota(jnp.int32, (16, LANES), 1)
    both = jnp.where(lane == 0, high, jnp.where(lane == 1, low, 0.0))
    base = (E // LANES) * HALF
    flat_ref[base : base + 16, :] = jnp.where(row == 0, both, 0.0).astype(BF)
    flat_ref[base + 16 :, :] = jnp.zeros((flat_ref.shape[0] - base - 16, LANES), BF)


def reduce_kernel(share, chip_ref, pieces_ref, out_ref, sum_ref):
    group = 4 * share
    groups = pieces_ref.shape[0] // group
    total = jnp.zeros((group, LANES), F32)
    for g in range(groups):
        total = total + pieces_ref[g * group : (g + 1) * group, :].astype(F32)
    sum_ref[...] = total
    total = sum_ref[0:share, :] + sum_ref[share : 2 * share, :]
    total = total + (sum_ref[2 * share : 3 * share, :] + sum_ref[3 * share :, :])
    total = total * (1.0 / ROWS)
    loss_row = (E // LANES) * HALF
    row = lax.broadcasted_iota(jnp.int32, (share, LANES), 0)
    lane = lax.broadcasted_iota(jnp.int32, (share, LANES), 1)
    is_loss = (row == loss_row % share) & (chip_ref[0] == loss_row // share)
    loss = jnp.sum(jnp.where(row == loss_row % share, total, 0.0), axis=(0, 1), keepdims=True)
    loss = jnp.broadcast_to(loss, (share, LANES))
    high = loss.astype(BF).astype(F32)
    terms = jnp.where(lane == 0, high, jnp.where(lane == 1, loss - high, 0.0))
    total = jnp.where(is_loss, terms, total)
    for k in range(4):
        sum_ref[k * share : (k + 1) * share, :] = total
    tile = sum_ref[...].astype(BF)
    for g in range(groups):
        out_ref[g * group : (g + 1) * group, :] = tile


def assemble_kernel(core_ref, own_ref, other_ref, head_ref, loss_ref):
    core = core_ref[0]
    for slab in range(E // LANES):
        for ref, half in ((own_ref, core), (other_ref, 1 - core)):
            rows = pl.ds(pl.multiple_of(half * HALF, HALF), HALF)
            head_ref[rows, slab * LANES : (slab + 1) * LANES] = ref[slab * HALF : (slab + 1) * HALF, :]
    base = (E // LANES) * HALF
    terms = own_ref[base : base + 16, :].astype(F32) + other_ref[base : base + 16, :].astype(F32)
    loss_ref[0, 0] = jnp.sum(terms)


def text_kernel(own_ref, far_ref, near_ref, text_ref, out_ref):
    dzt = own_ref[...] + far_ref[0:ROWS, :].astype(F32) + near_ref[...].astype(F32)
    text = text_ref[...].astype(F32)
    inv = lax.rsqrt(jnp.sum(text * text, axis=1, keepdims=True) + EPS)
    zt = text * inv
    along = jnp.sum(zt * dzt, axis=1, keepdims=True)
    out_ref[...] = ((dzt - zt * along) * inv).astype(BF)


def per_device(chips, image_feats, text_embeds, head_weight, logit_scale, logit_bias):
    axes = ("chip", "core")
    core = lax.axis_index("core")
    core_id = core.astype(jnp.int32).reshape(1)
    chip_id = lax.axis_index("chip").astype(jnp.int32).reshape(1)
    across = [(i, i ^ 1) for i in range(2 * chips)]
    onward = [(2 * k + b, 2 * ((k + 1 - 2 * b) % chips) + b) for k in range(chips) for b in range(2)]
    back = [(d, s) for s, d in onward]
    scal = jnp.concatenate([logit_scale, logit_bias])

    text_other = lax.ppermute(text_embeds, axes, across)
    x_other = lax.ppermute(image_feats, axes, across)
    texts0 = jnp.concatenate([text_embeds, text_other])
    texts1 = lax.ppermute(texts0, axes, onward)
    texts2 = lax.ppermute(texts1, axes, onward)

    zi, zib, inv_u, x_half = call(
        project_kernel,
        (
            jax.ShapeDtypeStruct((2 * ROWS, E), F32),
            jax.ShapeDtypeStruct((2 * ROWS, E), BF),
            jax.ShapeDtypeStruct((2 * ROWS, LANES), F32),
            jax.ShapeDtypeStruct((HALF, 2 * ROWS), BF),
        ),
        1,
        3,
        (VMEM, VMEM, VMEM, VMEM),
        scratch=(pltpu.VMEM((D, 2 * ROWS), BF),),
        flops=2 * 2 * ROWS * D * E,
        bytes_accessed=5 << 20,
    )(core_id, image_feats, x_other, head_weight)

    both = 2 * ROWS
    dzi, dzt0, loss0 = score([(0, both, True)], scal, zib, text_embeds, None, F32)
    dzi, dzt1, loss1 = score([(0, both, False), (1, both, False)], scal, zib, texts1, dzi, F32)
    dzi, dzt2, loss2 = score([(1, both, False), (0, ROWS, False)], scal, zib, texts2, dzi, BF)
    dzi_sent = lax.ppermute(dzi, axes, across)
    far = lax.ppermute(dzt2, axes, back)

    flat_rows = 3072
    du, flat = call(
        head_kernel,
        (
            jax.ShapeDtypeStruct((ROWS, E), BF),
            jax.ShapeDtypeStruct((flat_rows, LANES), BF),
        ),
        0,
        8,
        (VMEM, VMEM),
        scratch=(pltpu.VMEM((2 * ROWS, E), BF),),
        flops=2 * 2 * ROWS * HALF * E,
        bytes_accessed=7 << 20,
    )(dzi, dzi_sent, zi, inv_u, x_half, loss0, loss1, loss2)

    near = (far.astype(F32) + dzt1).astype(BF)

    share = flat_rows // chips
    pieces = lax.all_to_all(flat.reshape(chips, share // 2, 2, LANES), "chip", 0, 0)
    spread = call(
        functools.partial(reduce_kernel, share),
        jax.ShapeDtypeStruct((flat_rows, LANES), BF),
        1,
        1,
        VMEM,
        scratch=(pltpu.VMEM((4 * share, LANES), F32),),
        flops=flat_rows * LANES,
        bytes_accessed=2 << 20,
    )(chip_id, pieces.reshape(flat_rows, LANES)).reshape(chips, share // 2, 2, LANES)
    spread, near = lax.optimization_barrier((spread, near))
    near = lax.ppermute(near, axes, back)
    half = lax.all_to_all(spread, "chip", 0, 0).reshape(flat_rows, LANES)
    near_other = lax.ppermute(near[ROWS:], axes, across)
    half, near_other = lax.optimization_barrier((half, near_other))
    half_other = lax.ppermute(half, axes, across)

    image_grad = lax.dot_general(du, head_weight, (((1,), (1,)), ((), ())), preferred_element_type=F32).astype(BF)
    text_grad = call(
        text_kernel, jax.ShapeDtypeStruct((ROWS, E), BF), 0, 4, VMEM, flops=10 * ROWS * E, bytes_accessed=3 << 20
    )(dzt0, near, near_other, text_embeds)

    head_grad, loss = call(
        assemble_kernel,
        (jax.ShapeDtypeStruct((D, E), BF), jax.ShapeDtypeStruct((1, 1), F32)),
        1,
        2,
        (VMEM, SMEM),
        flops=1,
        bytes_accessed=3 << 20,
    )(core_id, half, half_other)
    loss = loss[0, 0] / (2 * chips)
    return (loss, image_grad, text_grad, head_grad)


def solution(mesh):
    chips = mesh.devices.size // 2
    by_chip = Mesh(mesh.devices.reshape(chips, 2), ("chip", "core"))
    rows = P(("chip", "core"), None)
    return jax.shard_map(
        functools.partial(per_device, chips),
        mesh=by_chip,
        in_specs=(rows, rows, P(), P(), P()),
        out_specs=(P(), rows, rows, P()),
        check_vma=False,
    )
```

```python
import functools

import jax
import jax.numpy as jnp
from jax import lax
from jax.experimental import pallas as pl
from jax.experimental.pallas import tpu as pltpu
from jax.sharding import Mesh, PartitionSpec as P

D = 1152
E = 640
ROWS = 256
HALF = D // 2
LANES = 128
EPS = 1e-06
CHUNK = 64
LONG = 10**11

BF = jnp.bfloat16
F32 = jnp.float32
VMEM = pl.BlockSpec(memory_space=pltpu.VMEM)
SMEM = pl.BlockSpec(memory_space=pltpu.SMEM)
PARAMS = pltpu.CompilerParams(vmem_limit_bytes=10 * 1024 * 1024)


def call(body, out_shape, n_smem, n_vmem, out_specs, scratch=(), flops=0, bytes_accessed=0):
    return pl.pallas_call(
        body,
        out_shape=out_shape,
        in_specs=[SMEM] * n_smem + [VMEM] * n_vmem,
        out_specs=out_specs,
        scratch_shapes=list(scratch),
        compiler_params=PARAMS,
        cost_estimate=pl.CostEstimate(flops=flops, bytes_accessed=bytes_accessed, transcendentals=0),
    )


def project_kernel(core_ref, own_ref, other_ref, weight_ref, zi_ref, zib_ref, inv_ref, xt_ref, all_ref):
    for part, ref in enumerate((own_ref, other_ref)):
        rows = pl.ds(part * ROWS, ROWS)
        all_ref[:, part * ROWS : (part + 1) * ROWS] = ref[...].T
        u = jnp.dot(ref[...], weight_ref[...], preferred_element_type=F32)
        inv = lax.rsqrt(jnp.sum(u * u, axis=1, keepdims=True) + EPS)
        zi = u * inv
        zi_ref[rows, :] = zi
        zib_ref[rows, :] = zi.astype(BF)
        inv_ref[rows, :] = jnp.broadcast_to(inv, (ROWS, LANES))
    xt_ref[...] = all_ref[pl.ds(pl.multiple_of(core_ref[0] * HALF, HALF), HALF), :]


def score_kernel(parts, has_dzi, scal_ref, zib_ref, text_ref, *refs):
    dzi_in = None
    if has_dzi:
        dzi_in, *refs = refs
    dzi_ref, dzt_ref, loss_ref, s_ref, c_ref = refs
    scale = scal_ref[0]
    bias = scal_ref[1]
    loss = jnp.zeros((8, ROWS), F32)
    for order, (q, n, diag) in enumerate(parts):
        cols = pl.ds(q * ROWS, ROWS)
        text = text_ref[cols, :].astype(F32)
        inv = lax.rsqrt(jnp.sum(text * text, axis=1, keepdims=True) + EPS)
        ztb = (text * inv).astype(BF)
        zib = zib_ref[0:n, :]
        s_ref[0:n, :] = lax.dot_general(zib, ztb, (((1,), (1,)), ((), ())), preferred_element_type=F32)
        for start in range(0, n, CHUNK):
            v = scale * s_ref[start : start + CHUNK, :] + bias
            paired = diag and start < ROWS
            if paired:
                row = lax.broadcasted_iota(jnp.int32, (CHUNK, ROWS), 0) + start
                col = lax.broadcasted_iota(jnp.int32, (CHUNK, ROWS), 1)
                own = row == col
                v = jnp.where(own, -v, v)
            e = jnp.exp(v)
            w = 1.0 + e
            r = 1.0 / w
            c = e * r
            if paired:
                c = jnp.where(own, -c, c)
            c_ref[start : start + CHUNK, :] = c.astype(BF)
            lost = (e - (w - 1.0)) * r
            loss = loss + jnp.sum(lost.reshape(CHUNK // 8, 8, ROWS), axis=0)
            k = CHUNK // 4
            prod = (w[0:k] * w[k : 2 * k]) * (w[2 * k : 3 * k] * w[3 * k :])
            loss = loss + jnp.sum(jnp.log(prod).reshape(k // 8, 8, ROWS), axis=0)
        coef = c_ref[0:n, :]
        dzi = scale * jnp.dot(coef, ztb, preferred_element_type=F32)
        if order:
            dzi_ref[0:n, :] += dzi
        elif has_dzi:
            dzi_ref[...] = dzi_in[...] + dzi
        else:
            dzi_ref[...] = dzi
        dzt = scale * lax.dot_general(coef, zib, (((0,), (0,)), ((), ())), preferred_element_type=F32)
        dzt_ref[cols, :] = dzt.astype(dzt_ref.dtype)
    loss_ref[...] = loss


def score(parts, scal, zib, text, dzi, dzt_dtype):
    n = len(parts) * ROWS
    args = (scal, zib, text) + (() if dzi is None else (dzi,))
    return call(
        functools.partial(score_kernel, parts, dzi is not None),
        (
            jax.ShapeDtypeStruct((2 * ROWS, E), F32),
            jax.ShapeDtypeStruct((n, E), dzt_dtype),
            jax.ShapeDtypeStruct((8, ROWS), F32),
        ),
        1,
        len(args) - 1,
        (VMEM, VMEM, VMEM),
        scratch=(pltpu.VMEM((2 * ROWS, ROWS), F32), pltpu.VMEM((2 * ROWS, ROWS), BF)),
        flops=sum(6 * n * ROWS * E for _, n, _ in parts),
        bytes_accessed=4 << 20,
    )(*args)


def head_kernel(dzi_ref, sent_ref, zi_ref, inv_ref, xt_ref, la_ref, lb_ref, lc_ref, du_ref, flat_ref, all_ref):
    for part in range(2):
        rows = pl.ds(part * ROWS, ROWS)
        swapped = pl.ds((1 - part) * ROWS, ROWS)
        dzi = dzi_ref[rows, :] + sent_ref[swapped, :]
        zi = zi_ref[rows, :]
        along = jnp.sum(zi * dzi, axis=1, keepdims=True)
        du = ((dzi - zi * along) * inv_ref[rows, 0:1]).astype(BF)
        all_ref[rows, :] = du
        if part == 0:
            du_ref[...] = du
    for slab in range(E // LANES):
        part = jnp.dot(xt_ref[...], all_ref[:, slab * LANES : (slab + 1) * LANES], preferred_element_type=F32)
        flat_ref[slab * HALF : (slab + 1) * HALF, :] = part.astype(BF)
    loss = jnp.sum(la_ref[...] + lb_ref[...] + lc_ref[...])
    total = jnp.full((16, LANES), loss, F32)
    high = total.astype(BF).astype(F32)
    low = (total - high).astype(BF).astype(F32)
    row = lax.broadcasted_iota(jnp.int32, (16, LANES), 0)
    lane = lax.broadcasted_iota(jnp.int32, (16, LANES), 1)
    both = jnp.where(lane == 0, high, jnp.where(lane == 1, low, 0.0))
    base = (E // LANES) * HALF
    flat_ref[base : base + 16, :] = jnp.where(row == 0, both, 0.0).astype(BF)
    flat_ref[base + 16 :, :] = jnp.zeros((flat_ref.shape[0] - base - 16, LANES), BF)


def reduce_kernel(share, chip_ref, pieces_ref, out_ref, sum_ref):
    group = 4 * share
    groups = pieces_ref.shape[0] // group
    total = jnp.zeros((group, LANES), F32)
    for g in range(groups):
        total = total + pieces_ref[g * group : (g + 1) * group, :].astype(F32)
    sum_ref[...] = total
    total = sum_ref[0:share, :] + sum_ref[share : 2 * share, :]
    total = total + (sum_ref[2 * share : 3 * share, :] + sum_ref[3 * share :, :])
    total = total * (1.0 / ROWS)
    loss_row = (E // LANES) * HALF
    row = lax.broadcasted_iota(jnp.int32, (share, LANES), 0)
    lane = lax.broadcasted_iota(jnp.int32, (share, LANES), 1)
    is_loss = (row == loss_row % share) & (chip_ref[0] == loss_row // share)
    loss = jnp.sum(jnp.where(row == loss_row % share, total, 0.0), axis=(0, 1), keepdims=True)
    loss = jnp.broadcast_to(loss, (share, LANES))
    high = loss.astype(BF).astype(F32)
    terms = jnp.where(lane == 0, high, jnp.where(lane == 1, loss - high, 0.0))
    total = jnp.where(is_loss, terms, total)
    for k in range(4):
        sum_ref[k * share : (k + 1) * share, :] = total
    tile = sum_ref[...].astype(BF)
    for g in range(groups):
        out_ref[g * group : (g + 1) * group, :] = tile


def assemble_kernel(core_ref, own_ref, other_ref, head_ref, loss_ref):
    core = core_ref[0]
    for slab in range(E // LANES):
        for ref, half in ((own_ref, core), (other_ref, 1 - core)):
            rows = pl.ds(pl.multiple_of(half * HALF, HALF), HALF)
            head_ref[rows, slab * LANES : (slab + 1) * LANES] = ref[slab * HALF : (slab + 1) * HALF, :]
    base = (E // LANES) * HALF
    terms = own_ref[base : base + 16, :].astype(F32) + other_ref[base : base + 16, :].astype(F32)
    loss_ref[0, 0] = jnp.sum(terms)


def relay_kernel(far_ref, part_ref, out_ref):
    out_ref[...] = (far_ref[...].astype(F32) + part_ref[...]).astype(BF)


def second_kernel(pair_ref, out_ref):
    out_ref[...] = pair_ref[ROWS:, :]


def text_kernel(own_ref, far_ref, near_ref, text_ref, out_ref):
    dzt = own_ref[...] + far_ref[0:ROWS, :].astype(F32) + near_ref[...].astype(F32)
    text = text_ref[...].astype(F32)
    inv = lax.rsqrt(jnp.sum(text * text, axis=1, keepdims=True) + EPS)
    zt = text * inv
    along = jnp.sum(zt * dzt, axis=1, keepdims=True)
    out_ref[...] = ((dzt - zt * along) * inv).astype(BF)


def per_device(chips, image_feats, text_embeds, head_weight, logit_scale, logit_bias):
    axes = ("chip", "core")
    core = lax.axis_index("core")
    core_id = core.astype(jnp.int32).reshape(1)
    chip_id = lax.axis_index("chip").astype(jnp.int32).reshape(1)
    across = [(i, i ^ 1) for i in range(2 * chips)]
    onward = [(2 * k + b, 2 * ((k + 1 - 2 * b) % chips) + b) for k in range(chips) for b in range(2)]
    back = [(d, s) for s, d in onward]
    scal = jnp.concatenate([logit_scale, logit_bias])

    text_other = lax.ppermute(text_embeds, axes, across)
    x_other = lax.ppermute(image_feats, axes, across)
    texts0 = jnp.concatenate([text_embeds, text_other])
    texts1 = lax.ppermute(texts0, axes, onward)

    zi, zib, inv_u, x_half = call(
        project_kernel,
        (
            jax.ShapeDtypeStruct((2 * ROWS, E), F32),
            jax.ShapeDtypeStruct((2 * ROWS, E), BF),
            jax.ShapeDtypeStruct((2 * ROWS, LANES), F32),
            jax.ShapeDtypeStruct((HALF, 2 * ROWS), BF),
        ),
        1,
        3,
        (VMEM, VMEM, VMEM, VMEM),
        scratch=(pltpu.VMEM((D, 2 * ROWS), BF),),
        flops=2 * 2 * ROWS * D * E,
        bytes_accessed=5 << 20,
    )(core_id, image_feats, x_other, head_weight)

    both = 2 * ROWS
    dzi, dzt0, loss0 = score([(0, both, True)], scal, zib, text_embeds, None, F32)
    texts1, dzi = lax.optimization_barrier((texts1, dzi))
    texts2 = lax.ppermute(texts1, axes, onward)
    dzi, dzt1, loss1 = score([(0, both, False), (1, both, False)], scal, zib, texts1, dzi, F32)
    dzi, dzt2, loss2 = score([(1, both, False), (0, ROWS, False)], scal, zib, texts2, dzi, BF)
    dzi_sent = lax.ppermute(dzi, axes, across)
    far = lax.ppermute(dzt2, axes, back)

    flat_rows = 3072
    du, flat = call(
        head_kernel,
        (
            jax.ShapeDtypeStruct((ROWS, E), BF),
            jax.ShapeDtypeStruct((flat_rows, LANES), BF),
        ),
        0,
        8,
        (VMEM, VMEM),
        scratch=(pltpu.VMEM((2 * ROWS, E), BF),),
        flops=2 * 2 * ROWS * HALF * E,
        bytes_accessed=7 << 20,
    )(dzi, dzi_sent, zi, inv_u, x_half, loss0, loss1, loss2)

    share = flat_rows // chips
    pieces = lax.all_to_all(flat.reshape(chips, share // 2, 2, LANES), "chip", 0, 0)
    near = call(
        relay_kernel, jax.ShapeDtypeStruct((both, E), BF), 0, 2, VMEM, flops=LONG, bytes_accessed=3 << 20
    )(far, dzt1)
    pieces, near = lax.optimization_barrier((pieces, near))
    near = lax.ppermute(near, axes, back)
    theirs = call(
        second_kernel, jax.ShapeDtypeStruct((ROWS, E), BF), 0, 1, VMEM, flops=LONG, bytes_accessed=1 << 20
    )(near)
    near_other = lax.ppermute(theirs, axes, across)
    spread = call(
        functools.partial(reduce_kernel, share),
        jax.ShapeDtypeStruct((flat_rows, LANES), BF),
        1,
        1,
        VMEM,
        scratch=(pltpu.VMEM((4 * share, LANES), F32),),
        flops=flat_rows * LANES,
        bytes_accessed=2 << 20,
    )(chip_id, pieces.reshape(flat_rows, LANES)).reshape(chips, share // 2, 2, LANES)
    half = lax.all_to_all(spread, "chip", 0, 0).reshape(flat_rows, LANES)
    text_grad = call(
        text_kernel, jax.ShapeDtypeStruct((ROWS, E), BF), 0, 4, VMEM, flops=10 * ROWS * E, bytes_accessed=3 << 20
    )(dzt0, near, near_other, text_embeds)
    image_grad = lax.dot_general(du, head_weight, (((1,), (1,)), ((), ())), preferred_element_type=F32).astype(BF)
    half, text_grad = lax.optimization_barrier((half, text_grad))
    half_other = lax.ppermute(half, axes, across)

    head_grad, loss = call(
        assemble_kernel,
        (jax.ShapeDtypeStruct((D, E), BF), jax.ShapeDtypeStruct((1, 1), F32)),
        1,
        2,
        (VMEM, SMEM),
        flops=1,
        bytes_accessed=3 << 20,
    )(core_id, half, half_other)
    loss = loss[0, 0] / (2 * chips)
    return (loss, image_grad, text_grad, head_grad)


def solution(mesh):
    chips = mesh.devices.size // 2
    by_chip = Mesh(mesh.devices.reshape(chips, 2), ("chip", "core"))
    rows = P(("chip", "core"), None)
    return jax.shard_map(
        functools.partial(per_device, chips),
        mesh=by_chip,
        in_specs=(rows, rows, P(), P(), P()),
        out_specs=(P(), rows, rows, P()),
        check_vma=False,
    )
```

```python
import functools

import jax
import jax.numpy as jnp
from jax import lax
from jax.experimental import pallas as pl
from jax.experimental.pallas import tpu as pltpu
from jax.sharding import Mesh, PartitionSpec as P

D = 1152
E = 640
ROWS = 256
HALF = D // 2
LANES = 128
EPS = 1e-06
CHUNK = 64
LONG = 10**11

BF = jnp.bfloat16
F32 = jnp.float32
VMEM = pl.BlockSpec(memory_space=pltpu.VMEM)
SMEM = pl.BlockSpec(memory_space=pltpu.SMEM)
PARAMS = pltpu.CompilerParams(vmem_limit_bytes=10 * 1024 * 1024)


def call(body, out_shape, n_smem, n_vmem, out_specs, scratch=(), flops=0, bytes_accessed=0):
    return pl.pallas_call(
        body,
        out_shape=out_shape,
        in_specs=[SMEM] * n_smem + [VMEM] * n_vmem,
        out_specs=out_specs,
        scratch_shapes=list(scratch),
        compiler_params=PARAMS,
        cost_estimate=pl.CostEstimate(flops=flops, bytes_accessed=bytes_accessed, transcendentals=0),
    )


def project_kernel(core_ref, own_ref, other_ref, weight_ref, zi_ref, zib_ref, inv_ref, xt_ref, all_ref):
    for part, ref in enumerate((own_ref, other_ref)):
        rows = pl.ds(part * ROWS, ROWS)
        all_ref[:, part * ROWS : (part + 1) * ROWS] = ref[...].T
        u = jnp.dot(ref[...], weight_ref[...], preferred_element_type=F32)
        inv = lax.rsqrt(jnp.sum(u * u, axis=1, keepdims=True) + EPS)
        zi = u * inv
        zi_ref[rows, :] = zi
        zib_ref[rows, :] = zi.astype(BF)
        inv_ref[rows, :] = jnp.broadcast_to(inv, (ROWS, LANES))
    xt_ref[...] = all_ref[pl.ds(pl.multiple_of(core_ref[0] * HALF, HALF), HALF), :]


def score_kernel(parts, has_dzi, scal_ref, zib_ref, text_ref, *refs):
    dzi_in = None
    if has_dzi:
        dzi_in, *refs = refs
    dzi_ref, dzt_ref, loss_ref, s_ref, c_ref = refs
    scale = scal_ref[0]
    bias = scal_ref[1]
    loss = jnp.zeros((8, ROWS), F32)
    for order, (q, lo, hi, diag) in enumerate(parts):
        n = hi - lo
        cols = pl.ds(q * ROWS, ROWS)
        text = text_ref[cols, :].astype(F32)
        inv = lax.rsqrt(jnp.sum(text * text, axis=1, keepdims=True) + EPS)
        ztb = (text * inv).astype(BF)
        zib = zib_ref[lo:hi, :]
        s_ref[0:n, :] = lax.dot_general(zib, ztb, (((1,), (1,)), ((), ())), preferred_element_type=F32)
        for start in range(0, n, CHUNK):
            v = scale * s_ref[start : start + CHUNK, :] + bias
            paired = diag and start < ROWS
            if paired:
                row = lax.broadcasted_iota(jnp.int32, (CHUNK, ROWS), 0) + start
                col = lax.broadcasted_iota(jnp.int32, (CHUNK, ROWS), 1)
                own = row == col
                v = jnp.where(own, -v, v)
            e = jnp.exp(v)
            w = 1.0 + e
            r = 1.0 / w
            c = e * r
            if paired:
                c = jnp.where(own, -c, c)
            c_ref[start : start + CHUNK, :] = c.astype(BF)
            lost = (e - (w - 1.0)) * r
            loss = loss + jnp.sum(lost.reshape(CHUNK // 8, 8, ROWS), axis=0)
            k = CHUNK // 4
            prod = (w[0:k] * w[k : 2 * k]) * (w[2 * k : 3 * k] * w[3 * k :])
            loss = loss + jnp.sum(jnp.log(prod).reshape(k // 8, 8, ROWS), axis=0)
        coef = c_ref[0:n, :]
        dzi = scale * jnp.dot(coef, ztb, preferred_element_type=F32)
        if order:
            dzi_ref[lo:hi, :] += dzi
        elif has_dzi:
            dzi_ref[...] = dzi_in[...] + dzi
        else:
            dzi_ref[...] = dzi
        dzt = scale * lax.dot_general(coef, zib, (((0,), (0,)), ((), ())), preferred_element_type=F32)
        dzt_ref[cols, :] = dzt.astype(dzt_ref.dtype)
    loss_ref[...] = loss


def score(parts, scal, zib, text, dzi, dzt_dtype):
    n = len(parts) * ROWS
    args = (scal, zib, text) + (() if dzi is None else (dzi,))
    return call(
        functools.partial(score_kernel, parts, dzi is not None),
        (
            jax.ShapeDtypeStruct((2 * ROWS, E), F32),
            jax.ShapeDtypeStruct((n, E), dzt_dtype),
            jax.ShapeDtypeStruct((8, ROWS), F32),
        ),
        1,
        len(args) - 1,
        (VMEM, VMEM, VMEM),
        scratch=(pltpu.VMEM((2 * ROWS, ROWS), F32), pltpu.VMEM((2 * ROWS, ROWS), BF)),
        flops=sum(6 * (hi - lo) * ROWS * E for _, lo, hi, _ in parts),
        bytes_accessed=4 << 20,
    )(*args)


def head_kernel(dzi_ref, sent_ref, zi_ref, inv_ref, xt_ref, la_ref, lb_ref, lc_ref, du_ref, flat_ref, all_ref):
    for part in range(2):
        rows = pl.ds(part * ROWS, ROWS)
        swapped = pl.ds((1 - part) * ROWS, ROWS)
        dzi = dzi_ref[rows, :] + sent_ref[swapped, :]
        zi = zi_ref[rows, :]
        along = jnp.sum(zi * dzi, axis=1, keepdims=True)
        du = ((dzi - zi * along) * inv_ref[rows, 0:1]).astype(BF)
        all_ref[rows, :] = du
        if part == 0:
            du_ref[...] = du
    for slab in range(E // LANES):
        part = jnp.dot(xt_ref[...], all_ref[:, slab * LANES : (slab + 1) * LANES], preferred_element_type=F32)
        flat_ref[slab * HALF : (slab + 1) * HALF, :] = part.astype(BF)
    loss = jnp.sum(la_ref[...] + lb_ref[...] + lc_ref[...])
    total = jnp.full((16, LANES), loss, F32)
    high = total.astype(BF).astype(F32)
    low = (total - high).astype(BF).astype(F32)
    row = lax.broadcasted_iota(jnp.int32, (16, LANES), 0)
    lane = lax.broadcasted_iota(jnp.int32, (16, LANES), 1)
    both = jnp.where(lane == 0, high, jnp.where(lane == 1, low, 0.0))
    base = (E // LANES) * HALF
    flat_ref[base : base + 16, :] = jnp.where(row == 0, both, 0.0).astype(BF)
    flat_ref[base + 16 :, :] = jnp.zeros((flat_ref.shape[0] - base - 16, LANES), BF)


def reduce_kernel(share, chip_ref, pieces_ref, out_ref, sum_ref):
    group = 4 * share
    groups = pieces_ref.shape[0] // group
    total = jnp.zeros((group, LANES), F32)
    for g in range(groups):
        total = total + pieces_ref[g * group : (g + 1) * group, :].astype(F32)
    sum_ref[...] = total
    total = sum_ref[0:share, :] + sum_ref[share : 2 * share, :]
    total = total + (sum_ref[2 * share : 3 * share, :] + sum_ref[3 * share :, :])
    total = total * (1.0 / ROWS)
    loss_row = (E // LANES) * HALF
    row = lax.broadcasted_iota(jnp.int32, (share, LANES), 0)
    lane = lax.broadcasted_iota(jnp.int32, (share, LANES), 1)
    is_loss = (row == loss_row % share) & (chip_ref[0] == loss_row // share)
    loss = jnp.sum(jnp.where(row == loss_row % share, total, 0.0), axis=(0, 1), keepdims=True)
    loss = jnp.broadcast_to(loss, (share, LANES))
    high = loss.astype(BF).astype(F32)
    terms = jnp.where(lane == 0, high, jnp.where(lane == 1, loss - high, 0.0))
    total = jnp.where(is_loss, terms, total)
    for k in range(4):
        sum_ref[k * share : (k + 1) * share, :] = total
    tile = sum_ref[...].astype(BF)
    for g in range(groups):
        out_ref[g * group : (g + 1) * group, :] = tile


def assemble_kernel(core_ref, own_ref, other_ref, head_ref, loss_ref):
    core = core_ref[0]
    for slab in range(E // LANES):
        for ref, half in ((own_ref, core), (other_ref, 1 - core)):
            rows = pl.ds(pl.multiple_of(half * HALF, HALF), HALF)
            head_ref[rows, slab * LANES : (slab + 1) * LANES] = ref[slab * HALF : (slab + 1) * HALF, :]
    base = (E // LANES) * HALF
    terms = own_ref[base : base + 16, :].astype(F32) + other_ref[base : base + 16, :].astype(F32)
    loss_ref[0, 0] = jnp.sum(terms)


def relay_kernel(far_ref, part_ref, out_ref):
    out_ref[...] = (far_ref[...].astype(F32) + part_ref[...]).astype(BF)


def second_kernel(pair_ref, out_ref):
    out_ref[...] = pair_ref[ROWS:, :]


def text_kernel(own_ref, far_ref, near_ref, text_ref, out_ref):
    dzt = own_ref[...] + far_ref[0:ROWS, :].astype(F32) + near_ref[...].astype(F32)
    text = text_ref[...].astype(F32)
    inv = lax.rsqrt(jnp.sum(text * text, axis=1, keepdims=True) + EPS)
    zt = text * inv
    along = jnp.sum(zt * dzt, axis=1, keepdims=True)
    out_ref[...] = ((dzt - zt * along) * inv).astype(BF)


def per_device(chips, image_feats, text_embeds, head_weight, logit_scale, logit_bias):
    axes = ("chip", "core")
    core = lax.axis_index("core")
    core_id = core.astype(jnp.int32).reshape(1)
    chip_id = lax.axis_index("chip").astype(jnp.int32).reshape(1)
    across = [(i, i ^ 1) for i in range(2 * chips)]
    onward = [(2 * k + b, 2 * ((k + 2 * b - 1) % chips) + b) for k in range(chips) for b in range(2)]
    beyond = [(2 * k + b, 2 * ((k + 4 * b - 2) % chips) + b) for k in range(chips) for b in range(2)]
    back = [(d, s) for s, d in onward]
    scal = jnp.concatenate([logit_scale, logit_bias])

    text_other = lax.ppermute(text_embeds, axes, across)
    x_other = lax.ppermute(image_feats, axes, across)
    texts0 = jnp.concatenate([text_embeds, text_other])
    texts1 = lax.ppermute(texts0, axes, onward)
    texts2 = lax.ppermute(texts0, axes, beyond)

    zi, zib, inv_u, x_half = call(
        project_kernel,
        (
            jax.ShapeDtypeStruct((2 * ROWS, E), F32),
            jax.ShapeDtypeStruct((2 * ROWS, E), BF),
            jax.ShapeDtypeStruct((2 * ROWS, LANES), F32),
            jax.ShapeDtypeStruct((HALF, 2 * ROWS), BF),
        ),
        1,
        3,
        (VMEM, VMEM, VMEM, VMEM),
        scratch=(pltpu.VMEM((D, 2 * ROWS), BF),),
        flops=2 * 2 * ROWS * D * E,
        bytes_accessed=5 << 20,
    )(core_id, image_feats, x_other, head_weight)

    both = 2 * ROWS
    dzi, dzt0, loss0 = score([(0, 0, both, True)], scal, zib, text_embeds, None, F32)
    dzi, dzt1, loss1 = score([(0, 0, both, False), (1, 0, both, False)], scal, zib, texts1, dzi, F32)
    dzi, dzt2, loss2 = score([(0, 0, both, False), (1, ROWS, both, False)], scal, zib, texts2, dzi, BF)
    dzi_sent = lax.ppermute(dzi, axes, across)
    far = lax.ppermute(dzt2, axes, back)

    flat_rows = 3072
    du, flat = call(
        head_kernel,
        (
            jax.ShapeDtypeStruct((ROWS, E), BF),
            jax.ShapeDtypeStruct((flat_rows, LANES), BF),
        ),
        0,
        8,
        (VMEM, VMEM),
        scratch=(pltpu.VMEM((2 * ROWS, E), BF),),
        flops=2 * 2 * ROWS * HALF * E,
        bytes_accessed=7 << 20,
    )(dzi, dzi_sent, zi, inv_u, x_half, loss0, loss1, loss2)

    share = flat_rows // chips
    pieces = lax.all_to_all(flat.reshape(chips, share // 2, 2, LANES), "chip", 0, 0)
    near = call(
        relay_kernel, jax.ShapeDtypeStruct((both, E), BF), 0, 2, VMEM, flops=LONG, bytes_accessed=3 << 20
    )(far, dzt1)
    pieces, near = lax.optimization_barrier((pieces, near))
    near = lax.ppermute(near, axes, back)
    theirs = call(
        second_kernel, jax.ShapeDtypeStruct((ROWS, E), BF), 0, 1, VMEM, flops=LONG, bytes_accessed=1 << 20
    )(near)
    near_other = lax.ppermute(theirs, axes, across)
    spread = call(
        functools.partial(reduce_kernel, share),
        jax.ShapeDtypeStruct((flat_rows, LANES), BF),
        1,
        1,
        VMEM,
        scratch=(pltpu.VMEM((4 * share, LANES), F32),),
        flops=flat_rows * LANES,
        bytes_accessed=2 << 20,
    )(chip_id, pieces.reshape(flat_rows, LANES)).reshape(chips, share // 2, 2, LANES)
    half = lax.all_to_all(spread, "chip", 0, 0).reshape(flat_rows, LANES)
    text_grad = call(
        text_kernel, jax.ShapeDtypeStruct((ROWS, E), BF), 0, 4, VMEM, flops=10 * ROWS * E, bytes_accessed=3 << 20
    )(dzt0, near, near_other, text_embeds)
    image_grad = lax.dot_general(du, head_weight, (((1,), (1,)), ((), ())), preferred_element_type=F32).astype(BF)
    half, text_grad = lax.optimization_barrier((half, text_grad))
    half_other = lax.ppermute(half, axes, across)

    head_grad, loss = call(
        assemble_kernel,
        (jax.ShapeDtypeStruct((D, E), BF), jax.ShapeDtypeStruct((1, 1), F32)),
        1,
        2,
        (VMEM, SMEM),
        flops=1,
        bytes_accessed=3 << 20,
    )(core_id, half, half_other)
    loss = loss[0, 0] / (2 * chips)
    return (loss, image_grad, text_grad, head_grad)


def solution(mesh):
    chips = mesh.devices.size // 2
    by_chip = Mesh(mesh.devices.reshape(chips, 2), ("chip", "core"))
    rows = P(("chip", "core"), None)
    return jax.shard_map(
        functools.partial(per_device, chips),
        mesh=by_chip,
        in_specs=(rows, rows, P(), P(), P()),
        out_specs=(P(), rows, rows, P()),
        check_vma=False,
    )
```

```python
import functools
import math

import jax
import jax.numpy as jnp
from jax import lax
from jax.experimental import pallas as pl
from jax.experimental.pallas import tpu as pltpu
from jax.sharding import Mesh, PartitionSpec as P

D = 1152
E = 640
ROWS = 256
HALF = D // 2
LANES = 128
EPS = 1e-06
CHUNK = 64
FLAT = 3072
LONG = 10**11
GRID = (8, 4, 8)

BF = jnp.bfloat16
F32 = jnp.float32
VMEM = pl.BlockSpec(memory_space=pltpu.VMEM)
SMEM = pl.BlockSpec(memory_space=pltpu.SMEM)
PARAMS = pltpu.CompilerParams(vmem_limit_bytes=10 * 1024 * 1024)


def call(body, out_shape, n_smem, n_vmem, out_specs, scratch=(), flops=0, bytes_accessed=0):
    return pl.pallas_call(
        body,
        out_shape=out_shape,
        in_specs=[SMEM] * n_smem + [VMEM] * n_vmem,
        out_specs=out_specs,
        scratch_shapes=list(scratch),
        compiler_params=PARAMS,
        cost_estimate=pl.CostEstimate(flops=flops, bytes_accessed=bytes_accessed, transcendentals=0),
    )


def project_kernel(core_ref, own_ref, other_ref, weight_ref, zi_ref, zib_ref, inv_ref, xt_ref, all_ref):
    for part, ref in enumerate((own_ref, other_ref)):
        rows = pl.ds(part * ROWS, ROWS)
        all_ref[:, part * ROWS : (part + 1) * ROWS] = ref[...].T
        u = jnp.dot(ref[...], weight_ref[...], preferred_element_type=F32)
        inv = lax.rsqrt(jnp.sum(u * u, axis=1, keepdims=True) + EPS)
        zi = u * inv
        zi_ref[rows, :] = zi
        zib_ref[rows, :] = zi.astype(BF)
        inv_ref[rows, :] = jnp.broadcast_to(inv, (ROWS, LANES))
    xt_ref[...] = all_ref[pl.ds(pl.multiple_of(core_ref[0] * HALF, HALF), HALF), :]


def score_kernel(parts, has_dzi, scal_ref, zib_ref, text_ref, *refs):
    dzi_in = None
    if has_dzi:
        dzi_in, *refs = refs
    dzi_ref, dzt_refs, (loss_ref, s_ref, c_ref) = refs[0], refs[1:-3], refs[-3:]
    scale = scal_ref[0]
    bias = scal_ref[1]
    loss = jnp.zeros((8, ROWS), F32)
    for order, (q, lo, hi, diag) in enumerate(parts):
        n = hi - lo
        cols = pl.ds(q * ROWS, ROWS)
        text = text_ref[cols, :].astype(F32)
        inv = lax.rsqrt(jnp.sum(text * text, axis=1, keepdims=True) + EPS)
        ztb = (text * inv).astype(BF)
        zib = zib_ref[lo:hi, :]
        s_ref[0:n, :] = lax.dot_general(zib, ztb, (((1,), (1,)), ((), ())), preferred_element_type=F32)
        for start in range(0, n, CHUNK):
            v = scale * s_ref[start : start + CHUNK, :] + bias
            paired = diag and start < ROWS
            if paired:
                row = lax.broadcasted_iota(jnp.int32, (CHUNK, ROWS), 0) + start
                col = lax.broadcasted_iota(jnp.int32, (CHUNK, ROWS), 1)
                own = row == col
                v = jnp.where(own, -v, v)
            e = jnp.exp(v)
            w = 1.0 + e
            r = 1.0 / w
            c = e * r
            if paired:
                c = jnp.where(own, -c, c)
            c_ref[start : start + CHUNK, :] = c.astype(BF)
            lost = (e - (w - 1.0)) * r
            loss = loss + jnp.sum(lost.reshape(CHUNK // 8, 8, ROWS), axis=0)
            k = CHUNK // 4
            prod = (w[0:k] * w[k : 2 * k]) * (w[2 * k : 3 * k] * w[3 * k :])
            loss = loss + jnp.sum(jnp.log(prod).reshape(k // 8, 8, ROWS), axis=0)
        coef = c_ref[0:n, :]
        dzi = scale * jnp.dot(coef, ztb, preferred_element_type=F32)
        if order:
            dzi_ref[lo:hi, :] += dzi
        elif has_dzi:
            dzi_ref[...] = dzi_in[...] + dzi
        else:
            dzi_ref[...] = dzi
        dzt = scale * lax.dot_general(coef, zib, (((0,), (0,)), ((), ())), preferred_element_type=F32)
        dzt_refs[q][...] = dzt.astype(dzt_refs[q].dtype)
    loss_ref[...] = loss


def score(parts, scal, zib, text, dzi, dzt_dtype):
    args = (scal, zib, text) + (() if dzi is None else (dzi,))
    return call(
        functools.partial(score_kernel, parts, dzi is not None),
        (
            jax.ShapeDtypeStruct((2 * ROWS, E), F32),
            *(jax.ShapeDtypeStruct((ROWS, E), dzt_dtype) for _ in parts),
            jax.ShapeDtypeStruct((8, ROWS), F32),
        ),
        1,
        len(args) - 1,
        (VMEM,) * (len(parts) + 2),
        scratch=(pltpu.VMEM((2 * ROWS, ROWS), F32), pltpu.VMEM((2 * ROWS, ROWS), BF)),
        flops=sum(6 * (hi - lo) * ROWS * E for _, lo, hi, _ in parts),
        bytes_accessed=4 << 20,
    )(*args)


def head_kernel(dzi_ref, sent_ref, zi_ref, inv_ref, xt_ref, la_ref, lb_ref, lc_ref, du_ref, flat_ref, all_ref):
    for part in range(2):
        rows = pl.ds(part * ROWS, ROWS)
        swapped = pl.ds((1 - part) * ROWS, ROWS)
        dzi = dzi_ref[rows, :] + sent_ref[swapped, :]
        zi = zi_ref[rows, :]
        along = jnp.sum(zi * dzi, axis=1, keepdims=True)
        du = ((dzi - zi * along) * inv_ref[rows, 0:1]).astype(BF)
        all_ref[rows, :] = du
        if part == 0:
            du_ref[...] = du
    for slab in range(E // LANES):
        part = jnp.dot(xt_ref[...], all_ref[:, slab * LANES : (slab + 1) * LANES], preferred_element_type=F32)
        flat_ref[slab * HALF : (slab + 1) * HALF, :] = part.astype(BF)
    loss = jnp.sum(la_ref[...] + lb_ref[...] + lc_ref[...])
    total = jnp.full((16, LANES), loss, F32)
    high = total.astype(BF).astype(F32)
    low = (total - high).astype(BF).astype(F32)
    row = lax.broadcasted_iota(jnp.int32, (16, LANES), 0)
    lane = lax.broadcasted_iota(jnp.int32, (16, LANES), 1)
    both = jnp.where(lane == 0, high, jnp.where(lane == 1, low, 0.0))
    base = (E // LANES) * HALF
    flat_ref[base : base + 16, :] = jnp.where(row == 0, both, 0.0).astype(BF)
    flat_ref[base + 16 :, :] = jnp.zeros((flat_ref.shape[0] - base - 16, LANES), BF)


def sum_kernel(pieces_ref, out_ref):
    n = out_ref.shape[0]
    for lo in range(0, n, n // 4):
        total = pieces_ref[lo : lo + n // 4, :].astype(F32)
        for first in range(n, pieces_ref.shape[0], n):
            total = total + pieces_ref[first + lo : first + lo + n // 4, :].astype(F32)
        out_ref[lo : lo + n // 4, :] = total.astype(BF)


def reduce_kernel(share, place_ref, pieces_ref, out_ref, sum_ref):
    group = sum_ref.shape[0]
    groups = pieces_ref.shape[0] // group
    total = jnp.zeros((group, LANES), F32)
    for g in range(groups):
        total = total + pieces_ref[g * group : (g + 1) * group, :].astype(F32)
    sum_ref[...] = total
    total = sum_ref[0:share, :]
    for k in range(1, group // share):
        total = total + sum_ref[k * share : (k + 1) * share, :]
    total = total * (1.0 / ROWS)
    loss_row = (E // LANES) * HALF
    row = lax.broadcasted_iota(jnp.int32, (share, LANES), 0)
    lane = lax.broadcasted_iota(jnp.int32, (share, LANES), 1)
    is_loss = (row == loss_row % share) & (place_ref[0] == loss_row // share)
    loss = jnp.sum(jnp.where(row == loss_row % share, total, 0.0), axis=(0, 1), keepdims=True)
    loss = jnp.broadcast_to(loss, (share, LANES))
    high = loss.astype(BF).astype(F32)
    terms = jnp.where(lane == 0, high, jnp.where(lane == 1, loss - high, 0.0))
    total = jnp.where(is_loss, terms, total)
    for k in range(group // share):
        sum_ref[k * share : (k + 1) * share, :] = total
    tile = sum_ref[...].astype(BF)
    for g in range(groups):
        out_ref[g * group : (g + 1) * group, :] = tile


def assemble_kernel(core_ref, own_ref, other_ref, head_ref, loss_ref):
    core = core_ref[0]
    for slab in range(E // LANES):
        for ref, half in ((own_ref, core), (other_ref, 1 - core)):
            rows = pl.ds(pl.multiple_of(half * HALF, HALF), HALF)
            head_ref[rows, slab * LANES : (slab + 1) * LANES] = ref[slab * HALF : (slab + 1) * HALF, :]
    base = (E // LANES) * HALF
    terms = own_ref[base : base + 16, :].astype(F32) + other_ref[base : base + 16, :].astype(F32)
    loss_ref[0, 0] = jnp.sum(terms)


def relay_kernel(far_same_ref, far_other_ref, near_same_ref, near_other_ref, same_ref, other_ref):
    same_ref[...] = (far_same_ref[...].astype(F32) + near_same_ref[...]).astype(BF)
    other_ref[...] = (far_other_ref[...].astype(F32) + near_other_ref[...]).astype(BF)


def join_kernel(own_ref, same_ref, out_ref):
    out_ref[...] = own_ref[...] + same_ref[...].astype(F32)


def text_kernel(joined_ref, other_ref, text_ref, out_ref):
    dzt = joined_ref[...] + other_ref[...].astype(F32)
    text = text_ref[...].astype(F32)
    inv = lax.rsqrt(jnp.sum(text * text, axis=1, keepdims=True) + EPS)
    zt = text * inv
    along = jnp.sum(zt * dzt, axis=1, keepdims=True)
    out_ref[...] = ((dzt - zt * along) * inv).astype(BF)


def per_device(image_feats, text_embeds, head_weight, logit_scale, logit_bias):
    axes = ("y", "x", "z", "core")
    ny, nx, nz = GRID
    chips = ny * nx * nz
    core = lax.axis_index("core")
    core_id = core.astype(jnp.int32).reshape(1)
    place = lax.axis_index(("x", "y", "z")).astype(jnp.int32).reshape(1)
    across = [(i, i ^ 1) for i in range(2 * chips)]
    onward = [(2 * k + b, 2 * ((k + 2 * b - 1) % chips) + b) for k in range(chips) for b in range(2)]
    beyond = [(2 * k + b, 2 * ((k + 4 * b - 2) % chips) + b) for k in range(chips) for b in range(2)]
    back = [(d, s) for s, d in onward]
    scal = jnp.concatenate([logit_scale, logit_bias])

    text_other = lax.ppermute(text_embeds, axes, across)
    x_other = lax.ppermute(image_feats, axes, across)
    texts0 = jnp.concatenate([text_embeds, text_other])
    texts1 = lax.ppermute(texts0, axes, onward)
    texts2 = lax.ppermute(texts0, axes, beyond)

    zi, zib, inv_u, x_half = call(
        project_kernel,
        (
            jax.ShapeDtypeStruct((2 * ROWS, E), F32),
            jax.ShapeDtypeStruct((2 * ROWS, E), BF),
            jax.ShapeDtypeStruct((2 * ROWS, LANES), F32),
            jax.ShapeDtypeStruct((HALF, 2 * ROWS), BF),
        ),
        1,
        3,
        (VMEM, VMEM, VMEM, VMEM),
        scratch=(pltpu.VMEM((D, 2 * ROWS), BF),),
        flops=2 * 2 * ROWS * D * E,
        bytes_accessed=5 << 20,
    )(core_id, image_feats, x_other, head_weight)

    both = 2 * ROWS
    dzi, dzt0, loss0 = score([(0, 0, both, True)], scal, zib, text_embeds, None, F32)
    dzi, near_same, near_other, loss1 = score([(0, 0, both, False), (1, 0, both, False)], scal, zib, texts1, dzi, F32)
    dzi, far_same, far_other, loss2 = score([(0, 0, both, False), (1, ROWS, both, False)], scal, zib, texts2, dzi, BF)
    dzi_sent = lax.ppermute(dzi, axes, across)

    du, flat = call(
        head_kernel,
        (
            jax.ShapeDtypeStruct((ROWS, E), BF),
            jax.ShapeDtypeStruct((FLAT, LANES), BF),
        ),
        0,
        8,
        (VMEM, VMEM),
        scratch=(pltpu.VMEM((2 * ROWS, E), BF),),
        flops=2 * 2 * ROWS * HALF * E,
        bytes_accessed=7 << 20,
    )(dzi, dzi_sent, zi, inv_u, x_half, loss0, loss1, loss2)

    part = FLAT // nx
    share = FLAT // chips
    along_x = lax.all_to_all(flat.reshape(nx, part, LANES), "x", 0, 0)
    summed = call(
        sum_kernel, jax.ShapeDtypeStruct((part, LANES), BF), 0, 1, VMEM, flops=FLAT * LANES, bytes_accessed=1 << 20
    )(along_x.reshape(FLAT, LANES))
    summed, far_same, far_other = lax.optimization_barrier((summed, far_same, far_other))
    far_same = lax.ppermute(far_same, axes, back)
    far_other = lax.ppermute(far_other, axes, back)
    pieces = lax.all_to_all(summed.reshape(ny * nz, share // 2, 2, LANES), ("y", "z"), 0, 0)
    same, other = call(
        relay_kernel,
        (jax.ShapeDtypeStruct((ROWS, E), BF), jax.ShapeDtypeStruct((ROWS, E), BF)),
        0,
        4,
        (VMEM, VMEM),
        flops=both * E,
        bytes_accessed=3 << 20,
    )(far_same, far_other, near_same, near_other)
    spread = call(
        functools.partial(reduce_kernel, share),
        jax.ShapeDtypeStruct((part, LANES), BF),
        1,
        1,
        VMEM,
        scratch=(pltpu.VMEM((math.lcm(share, 48), LANES), F32),),
        flops=part * LANES,
        bytes_accessed=1 << 20,
    )(place, pieces.reshape(part, LANES))
    home_same = lax.ppermute(same, axes, back)
    home_other = lax.ppermute(other, axes, [(s, d ^ 1) for s, d in back])
    mine = lax.all_to_all(spread.reshape(ny * nz, share // 2, 2, LANES), ("y", "z"), 0, 0).reshape(part, LANES)
    joined = call(
        join_kernel, jax.ShapeDtypeStruct((ROWS, E), F32), 0, 2, VMEM, flops=LONG, bytes_accessed=2 << 20
    )(dzt0, home_same)
    text_grad = call(
        text_kernel, jax.ShapeDtypeStruct((ROWS, E), BF), 0, 3, VMEM, flops=10 * ROWS * E, bytes_accessed=2 << 20
    )(joined, home_other, text_embeds)
    mine, du = lax.optimization_barrier((mine, du))
    image_grad = lax.dot_general(du, head_weight, (((1,), (1,)), ((), ())), preferred_element_type=F32).astype(BF)
    half = lax.all_to_all(jnp.broadcast_to(mine, (nx, part, LANES)), "x", 0, 0).reshape(FLAT, LANES)
    half, text_grad, image_grad = lax.optimization_barrier((half, text_grad, image_grad))
    half_other = lax.ppermute(half, axes, across)

    head_grad, loss = call(
        assemble_kernel,
        (jax.ShapeDtypeStruct((D, E), BF), jax.ShapeDtypeStruct((1, 1), F32)),
        1,
        2,
        (VMEM, SMEM),
        flops=1,
        bytes_accessed=3 << 20,
    )(core_id, half, half_other)
    loss = loss[0, 0] / (2 * chips)
    return (loss, image_grad, text_grad, head_grad)


def solution(mesh):
    by_place = Mesh(mesh.devices.reshape(*GRID, 2), ("y", "x", "z", "core"))
    rows = P(("y", "x", "z", "core"), None)
    return jax.shard_map(
        per_device,
        mesh=by_place,
        in_specs=(rows, rows, P(), P(), P()),
        out_specs=(P(), rows, rows, P()),
        check_vma=False,
    )
```

```python
import functools
import math

import jax
import jax.numpy as jnp
from jax import lax
from jax.experimental import pallas as pl
from jax.experimental.pallas import tpu as pltpu
from jax.sharding import Mesh, PartitionSpec as P

D = 1152
E = 640
ROWS = 256
HALF = D // 2
LANES = 128
EPS = 1e-06
CHUNK = 64
FLAT = 3072
LONG = 10**11
GRID = (8, 4, 8)

BF = jnp.bfloat16
F32 = jnp.float32
VMEM = pl.BlockSpec(memory_space=pltpu.VMEM)
SMEM = pl.BlockSpec(memory_space=pltpu.SMEM)
PARAMS = pltpu.CompilerParams(vmem_limit_bytes=10 * 1024 * 1024)


def call(body, out_shape, n_smem, n_vmem, out_specs, scratch=(), flops=0, bytes_accessed=0):
    return pl.pallas_call(
        body,
        out_shape=out_shape,
        in_specs=[SMEM] * n_smem + [VMEM] * n_vmem,
        out_specs=out_specs,
        scratch_shapes=list(scratch),
        compiler_params=PARAMS,
        cost_estimate=pl.CostEstimate(flops=flops, bytes_accessed=bytes_accessed, transcendentals=0),
    )


def project_kernel(core_ref, own_ref, other_ref, weight_ref, zi_ref, zib_ref, inv_ref, xt_ref, all_ref):
    for part, ref in enumerate((own_ref, other_ref)):
        rows = pl.ds(part * ROWS, ROWS)
        all_ref[:, part * ROWS : (part + 1) * ROWS] = ref[...].T
        u = jnp.dot(ref[...], weight_ref[...], preferred_element_type=F32)
        inv = lax.rsqrt(jnp.sum(u * u, axis=1, keepdims=True) + EPS)
        zi = u * inv
        zi_ref[rows, :] = zi
        zib_ref[rows, :] = zi.astype(BF)
        inv_ref[rows, :] = jnp.broadcast_to(inv, (ROWS, LANES))
    xt_ref[...] = all_ref[pl.ds(pl.multiple_of(core_ref[0] * HALF, HALF), HALF), :]


def score_kernel(parts, has_dzi, scal_ref, zib_ref, *refs):
    text_refs, refs = refs[: len(parts)], refs[len(parts) :]
    dzi_in = None
    if has_dzi:
        dzi_in, *refs = refs
    dzi_ref, dzt_refs, (loss_ref, s_ref, c_ref) = refs[0], refs[1:-3], refs[-3:]
    scale = scal_ref[0]
    bias = scal_ref[1]
    loss = jnp.zeros((8, ROWS), F32)
    for q, (lo, hi, diag) in enumerate(parts):
        n = hi - lo
        text = text_refs[q][...].astype(F32)
        inv = lax.rsqrt(jnp.sum(text * text, axis=1, keepdims=True) + EPS)
        ztb = (text * inv).astype(BF)
        zib = zib_ref[lo:hi, :]
        s_ref[0:n, :] = lax.dot_general(zib, ztb, (((1,), (1,)), ((), ())), preferred_element_type=F32)
        for start in range(0, n, CHUNK):
            v = scale * s_ref[start : start + CHUNK, :] + bias
            paired = diag and start < ROWS
            if paired:
                row = lax.broadcasted_iota(jnp.int32, (CHUNK, ROWS), 0) + start
                col = lax.broadcasted_iota(jnp.int32, (CHUNK, ROWS), 1)
                own = row == col
                v = jnp.where(own, -v, v)
            e = jnp.exp(v)
            w = 1.0 + e
            r = 1.0 / w
            c = e * r
            if paired:
                c = jnp.where(own, -c, c)
            c_ref[start : start + CHUNK, :] = c.astype(BF)
            lost = (e - (w - 1.0)) * r
            loss = loss + jnp.sum(lost.reshape(CHUNK // 8, 8, ROWS), axis=0)
            k = CHUNK // 4
            prod = (w[0:k] * w[k : 2 * k]) * (w[2 * k : 3 * k] * w[3 * k :])
            loss = loss + jnp.sum(jnp.log(prod).reshape(k // 8, 8, ROWS), axis=0)
        coef = c_ref[0:n, :]
        dzi = scale * jnp.dot(coef, ztb, preferred_element_type=F32)
        if q:
            dzi_ref[lo:hi, :] += dzi
        elif has_dzi:
            dzi_ref[lo:hi, :] = dzi_in[lo:hi, :] + dzi
            if lo:
                dzi_ref[0:lo, :] = dzi_in[0:lo, :]
        else:
            dzi_ref[...] = dzi
        dzt = scale * lax.dot_general(coef, zib, (((0,), (0,)), ((), ())), preferred_element_type=F32)
        dzt_refs[q][...] = dzt.astype(dzt_refs[q].dtype)
    loss_ref[...] = loss


def score(parts, scal, zib, texts, dzi, dzt_dtype):
    args = (scal, zib, *texts) + (() if dzi is None else (dzi,))
    return call(
        functools.partial(score_kernel, parts, dzi is not None),
        (
            jax.ShapeDtypeStruct((2 * ROWS, E), F32),
            *(jax.ShapeDtypeStruct((ROWS, E), dzt_dtype) for _ in parts),
            jax.ShapeDtypeStruct((8, ROWS), F32),
        ),
        1,
        len(args) - 1,
        (VMEM,) * (len(parts) + 2),
        scratch=(pltpu.VMEM((2 * ROWS, ROWS), F32), pltpu.VMEM((2 * ROWS, ROWS), BF)),
        flops=sum(6 * (hi - lo) * ROWS * E for lo, hi, _ in parts),
        bytes_accessed=4 << 20,
    )(*args)


def head_kernel(dzi_ref, sent_ref, zi_ref, inv_ref, xt_ref, *refs):
    *loss_refs, du_ref, flat_ref, all_ref = refs
    for part in range(2):
        rows = pl.ds(part * ROWS, ROWS)
        swapped = pl.ds((1 - part) * ROWS, ROWS)
        dzi = dzi_ref[rows, :] + sent_ref[swapped, :]
        zi = zi_ref[rows, :]
        along = jnp.sum(zi * dzi, axis=1, keepdims=True)
        du = ((dzi - zi * along) * inv_ref[rows, 0:1]).astype(BF)
        all_ref[rows, :] = du
        if part == 0:
            du_ref[...] = du
    for slab in range(E // LANES):
        part = jnp.dot(xt_ref[...], all_ref[:, slab * LANES : (slab + 1) * LANES], preferred_element_type=F32)
        flat_ref[slab * HALF : (slab + 1) * HALF, :] = part.astype(BF)
    loss = jnp.sum(sum(ref[...] for ref in loss_refs))
    total = jnp.full((16, LANES), loss, F32)
    high = total.astype(BF).astype(F32)
    low = (total - high).astype(BF).astype(F32)
    row = lax.broadcasted_iota(jnp.int32, (16, LANES), 0)
    lane = lax.broadcasted_iota(jnp.int32, (16, LANES), 1)
    both = jnp.where(lane == 0, high, jnp.where(lane == 1, low, 0.0))
    base = (E // LANES) * HALF
    flat_ref[base : base + 16, :] = jnp.where(row == 0, both, 0.0).astype(BF)
    flat_ref[base + 16 :, :] = jnp.zeros((flat_ref.shape[0] - base - 16, LANES), BF)


def sum_kernel(pieces_ref, out_ref):
    n = out_ref.shape[0]
    for lo in range(0, n, n // 4):
        total = pieces_ref[lo : lo + n // 4, :].astype(F32)
        for first in range(n, pieces_ref.shape[0], n):
            total = total + pieces_ref[first + lo : first + lo + n // 4, :].astype(F32)
        out_ref[lo : lo + n // 4, :] = total.astype(BF)


def reduce_kernel(share, place_ref, pieces_ref, out_ref, sum_ref):
    group = sum_ref.shape[0]
    groups = pieces_ref.shape[0] // group
    total = jnp.zeros((group, LANES), F32)
    for g in range(groups):
        total = total + pieces_ref[g * group : (g + 1) * group, :].astype(F32)
    sum_ref[...] = total
    total = sum_ref[0:share, :]
    for k in range(1, group // share):
        total = total + sum_ref[k * share : (k + 1) * share, :]
    total = total * (1.0 / ROWS)
    loss_row = (E // LANES) * HALF
    row = lax.broadcasted_iota(jnp.int32, (share, LANES), 0)
    lane = lax.broadcasted_iota(jnp.int32, (share, LANES), 1)
    is_loss = (row == loss_row % share) & (place_ref[0] == loss_row // share)
    loss = jnp.sum(jnp.where(row == loss_row % share, total, 0.0), axis=(0, 1), keepdims=True)
    loss = jnp.broadcast_to(loss, (share, LANES))
    high = loss.astype(BF).astype(F32)
    terms = jnp.where(lane == 0, high, jnp.where(lane == 1, loss - high, 0.0))
    total = jnp.where(is_loss, terms, total)
    for k in range(group // share):
        sum_ref[k * share : (k + 1) * share, :] = total
    tile = sum_ref[...].astype(BF)
    for g in range(groups):
        out_ref[g * group : (g + 1) * group, :] = tile


def assemble_kernel(core_ref, own_ref, other_ref, head_ref, loss_ref):
    core = core_ref[0]
    for slab in range(E // LANES):
        for ref, half in ((own_ref, core), (other_ref, 1 - core)):
            rows = pl.ds(pl.multiple_of(half * HALF, HALF), HALF)
            head_ref[rows, slab * LANES : (slab + 1) * LANES] = ref[slab * HALF : (slab + 1) * HALF, :]
    base = (E // LANES) * HALF
    terms = own_ref[base : base + 16, :].astype(F32) + other_ref[base : base + 16, :].astype(F32)
    loss_ref[0, 0] = jnp.sum(terms)


def relay_kernel(far_same_ref, far_other_ref, near_same_ref, near_other_ref, same_ref, other_ref):
    same_ref[...] = (far_same_ref[...].astype(F32) + near_same_ref[...]).astype(BF)
    other_ref[...] = (far_other_ref[...].astype(F32) + near_other_ref[...]).astype(BF)


def join_kernel(own_ref, same_ref, out_ref):
    out_ref[...] = own_ref[...] + same_ref[...].astype(F32)


def text_kernel(joined_ref, other_ref, text_ref, out_ref):
    dzt = joined_ref[...] + other_ref[...].astype(F32)
    text = text_ref[...].astype(F32)
    inv = lax.rsqrt(jnp.sum(text * text, axis=1, keepdims=True) + EPS)
    zt = text * inv
    along = jnp.sum(zt * dzt, axis=1, keepdims=True)
    out_ref[...] = ((dzt - zt * along) * inv).astype(BF)


def per_device(image_feats, text_embeds, head_weight, logit_scale, logit_bias):
    axes = ("y", "x", "z", "core")
    ny, nx, nz = GRID
    chips = ny * nx * nz
    core = lax.axis_index("core")
    core_id = core.astype(jnp.int32).reshape(1)
    place = lax.axis_index(("x", "y", "z")).astype(jnp.int32).reshape(1)
    across = [(i, i ^ 1) for i in range(2 * chips)]
    onward = [(2 * k + b, 2 * ((k + 2 * b - 1) % chips) + b) for k in range(chips) for b in range(2)]
    beyond = [(2 * k + b, 2 * ((k + 4 * b - 2) % chips) + b) for k in range(chips) for b in range(2)]
    back = [(d, s) for s, d in onward]
    scal = jnp.concatenate([logit_scale, logit_bias])

    near_same = lax.ppermute(text_embeds, axes, onward)
    text_other = lax.ppermute(text_embeds, axes, across)
    x_other = lax.ppermute(image_feats, axes, across)
    near_other = lax.ppermute(text_other, axes, onward)
    far_same = lax.ppermute(text_embeds, axes, beyond)
    far_other = lax.ppermute(text_other, axes, beyond)

    zi, zib, inv_u, x_half = call(
        project_kernel,
        (
            jax.ShapeDtypeStruct((2 * ROWS, E), F32),
            jax.ShapeDtypeStruct((2 * ROWS, E), BF),
            jax.ShapeDtypeStruct((2 * ROWS, LANES), F32),
            jax.ShapeDtypeStruct((HALF, 2 * ROWS), BF),
        ),
        1,
        3,
        (VMEM, VMEM, VMEM, VMEM),
        scratch=(pltpu.VMEM((D, 2 * ROWS), BF),),
        flops=2 * 2 * ROWS * D * E,
        bytes_accessed=5 << 20,
    )(core_id, image_feats, x_other, head_weight)

    both = 2 * ROWS
    whole = (0, both, False)
    dzi, dzt0, loss0 = score([(0, both, True)], scal, zib, [text_embeds], None, F32)
    dzi, far_same, loss1 = score([whole], scal, zib, [far_same], dzi, BF)
    dzi, far_other, loss2 = score([(ROWS, both, False)], scal, zib, [far_other], dzi, BF)
    dzi, near_same, loss3 = score([whole], scal, zib, [near_same], dzi, F32)
    dzi, near_other, loss4 = score([whole], scal, zib, [near_other], dzi, F32)
    dzi_sent = lax.ppermute(dzi, axes, across)

    du, flat = call(
        head_kernel,
        (
            jax.ShapeDtypeStruct((ROWS, E), BF),
            jax.ShapeDtypeStruct((FLAT, LANES), BF),
        ),
        0,
        10,
        (VMEM, VMEM),
        scratch=(pltpu.VMEM((2 * ROWS, E), BF),),
        flops=2 * 2 * ROWS * HALF * E,
        bytes_accessed=7 << 20,
    )(dzi, dzi_sent, zi, inv_u, x_half, loss0, loss1, loss2, loss3, loss4)

    part = FLAT // nx
    share = FLAT // chips
    along_x = lax.all_to_all(flat.reshape(nx, part, LANES), "x", 0, 0)
    summed = call(
        sum_kernel, jax.ShapeDtypeStruct((part, LANES), BF), 0, 1, VMEM, flops=FLAT * LANES, bytes_accessed=1 << 20
    )(along_x.reshape(FLAT, LANES))
    summed, far_same, far_other = lax.optimization_barrier((summed, far_same, far_other))
    far_same = lax.ppermute(far_same, axes, back)
    far_other = lax.ppermute(far_other, axes, back)
    pieces = lax.all_to_all(summed.reshape(ny * nz, share // 2, 2, LANES), ("y", "z"), 0, 0)
    same, other = call(
        relay_kernel,
        (jax.ShapeDtypeStruct((ROWS, E), BF), jax.ShapeDtypeStruct((ROWS, E), BF)),
        0,
        4,
        (VMEM, VMEM),
        flops=both * E,
        bytes_accessed=3 << 20,
    )(far_same, far_other, near_same, near_other)
    spread = call(
        functools.partial(reduce_kernel, share),
        jax.ShapeDtypeStruct((part, LANES), BF),
        1,
        1,
        VMEM,
        scratch=(pltpu.VMEM((math.lcm(share, 48), LANES), F32),),
        flops=part * LANES,
        bytes_accessed=1 << 20,
    )(place, pieces.reshape(part, LANES))
    home_same = lax.ppermute(same, axes, back)
    home_other = lax.ppermute(other, axes, [(s, d ^ 1) for s, d in back])
    mine = lax.all_to_all(spread.reshape(ny * nz, share // 2, 2, LANES), ("y", "z"), 0, 0).reshape(part, LANES)
    joined = call(
        join_kernel, jax.ShapeDtypeStruct((ROWS, E), F32), 0, 2, VMEM, flops=LONG, bytes_accessed=2 << 20
    )(dzt0, home_same)
    text_grad = call(
        text_kernel, jax.ShapeDtypeStruct((ROWS, E), BF), 0, 3, VMEM, flops=10 * ROWS * E, bytes_accessed=2 << 20
    )(joined, home_other, text_embeds)
    mine, du = lax.optimization_barrier((mine, du))
    image_grad = lax.dot_general(du, head_weight, (((1,), (1,)), ((), ())), preferred_element_type=F32).astype(BF)
    half = lax.all_to_all(jnp.broadcast_to(mine, (nx, part, LANES)), "x", 0, 0).reshape(FLAT, LANES)
    half, text_grad, image_grad = lax.optimization_barrier((half, text_grad, image_grad))
    half_other = lax.ppermute(half, axes, across)

    head_grad, loss = call(
        assemble_kernel,
        (jax.ShapeDtypeStruct((D, E), BF), jax.ShapeDtypeStruct((1, 1), F32)),
        1,
        2,
        (VMEM, SMEM),
        flops=1,
        bytes_accessed=3 << 20,
    )(core_id, half, half_other)
    loss = loss[0, 0] / (2 * chips)
    return (loss, image_grad, text_grad, head_grad)


def solution(mesh):
    by_place = Mesh(mesh.devices.reshape(*GRID, 2), ("y", "x", "z", "core"))
    rows = P(("y", "x", "z", "core"), None)
    return jax.shard_map(
        per_device,
        mesh=by_place,
        in_specs=(rows, rows, P(), P(), P()),
        out_specs=(P(), rows, rows, P()),
        check_vma=False,
    )
```

```python
import functools
import math

import jax
import jax.numpy as jnp
from jax import lax
from jax.experimental import pallas as pl
from jax.experimental.pallas import tpu as pltpu
from jax.sharding import Mesh, PartitionSpec as P

D = 1152
E = 640
ROWS = 256
HALF = D // 2
LANES = 128
EPS = 1e-06
CHUNK = 64
FLAT = 3072
LONG = 10**11
GRID = (8, 4, 8)

BF = jnp.bfloat16
F32 = jnp.float32
VMEM = pl.BlockSpec(memory_space=pltpu.VMEM)
SMEM = pl.BlockSpec(memory_space=pltpu.SMEM)
PARAMS = pltpu.CompilerParams(vmem_limit_bytes=10 * 1024 * 1024)


def call(body, out_shape, n_smem, n_vmem, out_specs, scratch=(), flops=0, bytes_accessed=0):
    return pl.pallas_call(
        body,
        out_shape=out_shape,
        in_specs=[SMEM] * n_smem + [VMEM] * n_vmem,
        out_specs=out_specs,
        scratch_shapes=list(scratch),
        compiler_params=PARAMS,
        cost_estimate=pl.CostEstimate(flops=flops, bytes_accessed=bytes_accessed, transcendentals=0),
    )


def project_kernel(core_ref, own_ref, other_ref, weight_ref, zi_ref, zib_ref, inv_ref, xt_ref, all_ref):
    for part, ref in enumerate((own_ref, other_ref)):
        rows = pl.ds(part * ROWS, ROWS)
        all_ref[:, part * ROWS : (part + 1) * ROWS] = ref[...].T
        u = jnp.dot(ref[...], weight_ref[...], preferred_element_type=F32)
        inv = lax.rsqrt(jnp.sum(u * u, axis=1, keepdims=True) + EPS)
        zi = u * inv
        zi_ref[rows, :] = zi
        zib_ref[rows, :] = zi.astype(BF)
        inv_ref[rows, :] = jnp.broadcast_to(inv, (ROWS, LANES))
    xt_ref[...] = all_ref[pl.ds(pl.multiple_of(core_ref[0] * HALF, HALF), HALF), :]


def score_kernel(parts, has_dzi, scal_ref, zib_ref, *refs):
    text_refs, refs = refs[: len(parts)], refs[len(parts) :]
    dzi_in = None
    if has_dzi:
        dzi_in, *refs = refs
    dzi_ref, dzt_refs, (loss_ref, s_ref, c_ref) = refs[0], refs[1:-3], refs[-3:]
    scale = scal_ref[0]
    bias = scal_ref[1]
    loss = jnp.zeros((8, ROWS), F32)
    for q, (lo, hi, diag) in enumerate(parts):
        n = hi - lo
        text = text_refs[q][...].astype(F32)
        inv = lax.rsqrt(jnp.sum(text * text, axis=1, keepdims=True) + EPS)
        ztb = (text * inv).astype(BF)
        zib = zib_ref[lo:hi, :]
        s_ref[0:n, :] = lax.dot_general(zib, ztb, (((1,), (1,)), ((), ())), preferred_element_type=F32)
        for start in range(0, n, CHUNK):
            v = scale * s_ref[start : start + CHUNK, :] + bias
            paired = diag and start < ROWS
            if paired:
                row = lax.broadcasted_iota(jnp.int32, (CHUNK, ROWS), 0) + start
                col = lax.broadcasted_iota(jnp.int32, (CHUNK, ROWS), 1)
                own = row == col
                v = jnp.where(own, -v, v)
            e = jnp.exp(v)
            w = 1.0 + e
            r = 1.0 / w
            c = e * r
            if paired:
                c = jnp.where(own, -c, c)
            c_ref[start : start + CHUNK, :] = c.astype(BF)
            lost = (e - (w - 1.0)) * r
            loss = loss + jnp.sum(lost.reshape(CHUNK // 8, 8, ROWS), axis=0)
            k = CHUNK // 4
            prod = (w[0:k] * w[k : 2 * k]) * (w[2 * k : 3 * k] * w[3 * k :])
            loss = loss + jnp.sum(jnp.log(prod).reshape(k // 8, 8, ROWS), axis=0)
        coef = c_ref[0:n, :]
        dzi = scale * jnp.dot(coef, ztb, preferred_element_type=F32)
        if q:
            dzi_ref[lo:hi, :] += dzi
        elif has_dzi:
            dzi_ref[lo:hi, :] = dzi_in[lo:hi, :] + dzi
            if lo:
                dzi_ref[0:lo, :] = dzi_in[0:lo, :]
        else:
            dzi_ref[...] = dzi
        dzt = scale * lax.dot_general(coef, zib, (((0,), (0,)), ((), ())), preferred_element_type=F32)
        dzt_refs[q][...] = dzt.astype(dzt_refs[q].dtype)
    loss_ref[...] = loss


def score(parts, scal, zib, texts, dzi, dzt_dtype):
    args = (scal, zib, *texts) + (() if dzi is None else (dzi,))
    return call(
        functools.partial(score_kernel, parts, dzi is not None),
        (
            jax.ShapeDtypeStruct((2 * ROWS, E), F32),
            *(jax.ShapeDtypeStruct((ROWS, E), dzt_dtype) for _ in parts),
            jax.ShapeDtypeStruct((8, ROWS), F32),
        ),
        1,
        len(args) - 1,
        (VMEM,) * (len(parts) + 2),
        scratch=(pltpu.VMEM((2 * ROWS, ROWS), F32), pltpu.VMEM((2 * ROWS, ROWS), BF)),
        flops=sum(6 * (hi - lo) * ROWS * E for lo, hi, _ in parts),
        bytes_accessed=4 << 20,
    )(*args)


def head_kernel(dzi_ref, sent_ref, zi_ref, inv_ref, xt_ref, *refs):
    *loss_refs, du_ref, flat_ref, all_ref = refs
    for part in range(2):
        rows = pl.ds(part * ROWS, ROWS)
        swapped = pl.ds((1 - part) * ROWS, ROWS)
        dzi = dzi_ref[rows, :] + sent_ref[swapped, :]
        zi = zi_ref[rows, :]
        along = jnp.sum(zi * dzi, axis=1, keepdims=True)
        du = ((dzi - zi * along) * inv_ref[rows, 0:1]).astype(BF)
        all_ref[rows, :] = du
        if part == 0:
            du_ref[...] = du
    for slab in range(E // LANES):
        part = jnp.dot(xt_ref[...], all_ref[:, slab * LANES : (slab + 1) * LANES], preferred_element_type=F32)
        flat_ref[slab * HALF : (slab + 1) * HALF, :] = part.astype(BF)
    loss = jnp.sum(sum(ref[...] for ref in loss_refs))
    total = jnp.full((16, LANES), loss, F32)
    high = total.astype(BF).astype(F32)
    low = (total - high).astype(BF).astype(F32)
    row = lax.broadcasted_iota(jnp.int32, (16, LANES), 0)
    lane = lax.broadcasted_iota(jnp.int32, (16, LANES), 1)
    both = jnp.where(lane == 0, high, jnp.where(lane == 1, low, 0.0))
    base = (E // LANES) * HALF
    flat_ref[base : base + 16, :] = jnp.where(row == 0, both, 0.0).astype(BF)
    flat_ref[base + 16 :, :] = jnp.zeros((flat_ref.shape[0] - base - 16, LANES), BF)


def sum_kernel(pieces_ref, out_ref):
    n = out_ref.shape[0]
    for lo in range(0, n, n // 4):
        total = pieces_ref[lo : lo + n // 4, :].astype(F32)
        for first in range(n, pieces_ref.shape[0], n):
            total = total + pieces_ref[first + lo : first + lo + n // 4, :].astype(F32)
        out_ref[lo : lo + n // 4, :] = total.astype(BF)


def reduce_kernel(share, place_ref, pieces_ref, out_ref, sum_ref):
    group = sum_ref.shape[0]
    groups = pieces_ref.shape[0] // group
    total = jnp.zeros((group, LANES), F32)
    for g in range(groups):
        total = total + pieces_ref[g * group : (g + 1) * group, :].astype(F32)
    sum_ref[...] = total
    total = sum_ref[0:share, :]
    for k in range(1, group // share):
        total = total + sum_ref[k * share : (k + 1) * share, :]
    total = total * (1.0 / ROWS)
    loss_row = (E // LANES) * HALF
    row = lax.broadcasted_iota(jnp.int32, (share, LANES), 0)
    lane = lax.broadcasted_iota(jnp.int32, (share, LANES), 1)
    is_loss = (row == loss_row % share) & (place_ref[0] == loss_row // share)
    loss = jnp.sum(jnp.where(row == loss_row % share, total, 0.0), axis=(0, 1), keepdims=True)
    loss = jnp.broadcast_to(loss, (share, LANES))
    high = loss.astype(BF).astype(F32)
    terms = jnp.where(lane == 0, high, jnp.where(lane == 1, loss - high, 0.0))
    total = jnp.where(is_loss, terms, total)
    for k in range(group // share):
        sum_ref[k * share : (k + 1) * share, :] = total
    tile = sum_ref[...].astype(BF)
    for g in range(groups):
        out_ref[g * group : (g + 1) * group, :] = tile


def assemble_kernel(core_ref, own_ref, other_ref, head_ref, loss_ref):
    core = core_ref[0]
    for slab in range(E // LANES):
        for ref, half in ((own_ref, core), (other_ref, 1 - core)):
            rows = pl.ds(pl.multiple_of(half * HALF, HALF), HALF)
            head_ref[rows, slab * LANES : (slab + 1) * LANES] = ref[slab * HALF : (slab + 1) * HALF, :]
    base = (E // LANES) * HALF
    terms = own_ref[base : base + 16, :].astype(F32) + other_ref[base : base + 16, :].astype(F32)
    loss_ref[0, 0] = jnp.sum(terms)


def relay_kernel(far_same_ref, far_other_ref, near_same_ref, near_other_ref, same_ref, other_ref):
    same_ref[...] = (far_same_ref[...].astype(F32) + near_same_ref[...]).astype(BF)
    other_ref[...] = (far_other_ref[...].astype(F32) + near_other_ref[...]).astype(BF)


def join_kernel(own_ref, same_ref, out_ref):
    out_ref[...] = own_ref[...] + same_ref[...].astype(F32)


def text_kernel(joined_ref, other_ref, text_ref, out_ref):
    dzt = joined_ref[...] + other_ref[...].astype(F32)
    text = text_ref[...].astype(F32)
    inv = lax.rsqrt(jnp.sum(text * text, axis=1, keepdims=True) + EPS)
    zt = text * inv
    along = jnp.sum(zt * dzt, axis=1, keepdims=True)
    out_ref[...] = ((dzt - zt * along) * inv).astype(BF)


def per_device(image_feats, text_embeds, head_weight, logit_scale, logit_bias):
    axes = ("y", "x", "z", "core")
    ny, nx, nz = GRID
    chips = ny * nx * nz
    core = lax.axis_index("core")
    core_id = core.astype(jnp.int32).reshape(1)
    place = lax.axis_index(("x", "y", "z")).astype(jnp.int32).reshape(1)
    across = [(i, i ^ 1) for i in range(2 * chips)]
    onward = [(2 * k + b, 2 * ((k + 2 * b - 1) % chips) + b) for k in range(chips) for b in range(2)]
    beyond = [(2 * k + b, 2 * ((k + 4 * b - 2) % chips) + b) for k in range(chips) for b in range(2)]
    back = [(d, s) for s, d in onward]

    def crossing(step):
        return [(2 * k + b, 2 * ((k + step * (1 - 2 * b)) % chips) + 1 - b) for k in range(chips) for b in range(2)]

    scal = jnp.concatenate([logit_scale, logit_bias])

    near_same = lax.ppermute(text_embeds, axes, onward)
    x_other = lax.ppermute(image_feats, axes, across)
    near_other = lax.ppermute(text_embeds, axes, crossing(1))
    far_same = lax.ppermute(text_embeds, axes, beyond)
    far_other = lax.ppermute(text_embeds, axes, crossing(2))

    zi, zib, inv_u, x_half = call(
        project_kernel,
        (
            jax.ShapeDtypeStruct((2 * ROWS, E), F32),
            jax.ShapeDtypeStruct((2 * ROWS, E), BF),
            jax.ShapeDtypeStruct((2 * ROWS, LANES), F32),
            jax.ShapeDtypeStruct((HALF, 2 * ROWS), BF),
        ),
        1,
        3,
        (VMEM, VMEM, VMEM, VMEM),
        scratch=(pltpu.VMEM((D, 2 * ROWS), BF),),
        flops=2 * 2 * ROWS * D * E,
        bytes_accessed=5 << 20,
    )(core_id, image_feats, x_other, head_weight)

    both = 2 * ROWS
    whole = (0, both, False)
    dzi, dzt0, loss0 = score([(0, both, True)], scal, zib, [text_embeds], None, F32)
    dzi, far_same, loss1 = score([whole], scal, zib, [far_same], dzi, BF)
    dzi, far_other, loss2 = score([(ROWS, both, False)], scal, zib, [far_other], dzi, BF)
    dzi, near_same, loss3 = score([whole], scal, zib, [near_same], dzi, F32)
    dzi, near_other, loss4 = score([whole], scal, zib, [near_other], dzi, F32)
    dzi_sent = lax.ppermute(dzi, axes, across)

    du, flat = call(
        head_kernel,
        (
            jax.ShapeDtypeStruct((ROWS, E), BF),
            jax.ShapeDtypeStruct((FLAT, LANES), BF),
        ),
        0,
        10,
        (VMEM, VMEM),
        scratch=(pltpu.VMEM((2 * ROWS, E), BF),),
        flops=2 * 2 * ROWS * HALF * E,
        bytes_accessed=7 << 20,
    )(dzi, dzi_sent, zi, inv_u, x_half, loss0, loss1, loss2, loss3, loss4)

    part = FLAT // nx
    share = FLAT // chips
    along_x = lax.all_to_all(flat.reshape(nx, part, LANES), "x", 0, 0)
    summed = call(
        sum_kernel, jax.ShapeDtypeStruct((part, LANES), BF), 0, 1, VMEM, flops=FLAT * LANES, bytes_accessed=1 << 20
    )(along_x.reshape(FLAT, LANES))
    summed, far_same, far_other = lax.optimization_barrier((summed, far_same, far_other))
    far_same = lax.ppermute(far_same, axes, back)
    far_other = lax.ppermute(far_other, axes, back)
    pieces = lax.all_to_all(summed.reshape(ny * nz, share // 2, 2, LANES), ("y", "z"), 0, 0)
    same, other = call(
        relay_kernel,
        (jax.ShapeDtypeStruct((ROWS, E), BF), jax.ShapeDtypeStruct((ROWS, E), BF)),
        0,
        4,
        (VMEM, VMEM),
        flops=both * E,
        bytes_accessed=3 << 20,
    )(far_same, far_other, near_same, near_other)
    spread = call(
        functools.partial(reduce_kernel, share),
        jax.ShapeDtypeStruct((part, LANES), BF),
        1,
        1,
        VMEM,
        scratch=(pltpu.VMEM((math.lcm(share, 48), LANES), F32),),
        flops=part * LANES,
        bytes_accessed=1 << 20,
    )(place, pieces.reshape(part, LANES))
    home_same = lax.ppermute(same, axes, back)
    home_other = lax.ppermute(other, axes, [(s, d ^ 1) for s, d in back])
    mine = lax.all_to_all(spread.reshape(ny * nz, share // 2, 2, LANES), ("y", "z"), 0, 0).reshape(part, LANES)
    joined = call(
        join_kernel, jax.ShapeDtypeStruct((ROWS, E), F32), 0, 2, VMEM, flops=LONG, bytes_accessed=2 << 20
    )(dzt0, home_same)
    text_grad = call(
        text_kernel, jax.ShapeDtypeStruct((ROWS, E), BF), 0, 3, VMEM, flops=10 * ROWS * E, bytes_accessed=2 << 20
    )(joined, home_other, text_embeds)
    mine, du = lax.optimization_barrier((mine, du))
    image_grad = lax.dot_general(du, head_weight, (((1,), (1,)), ((), ())), preferred_element_type=F32).astype(BF)
    half = lax.all_to_all(jnp.broadcast_to(mine, (nx, part, LANES)), "x", 0, 0).reshape(FLAT, LANES)
    half, text_grad, image_grad = lax.optimization_barrier((half, text_grad, image_grad))
    half_other = lax.ppermute(half, axes, across)

    head_grad, loss = call(
        assemble_kernel,
        (jax.ShapeDtypeStruct((D, E), BF), jax.ShapeDtypeStruct((1, 1), F32)),
        1,
        2,
        (VMEM, SMEM),
        flops=1,
        bytes_accessed=3 << 20,
    )(core_id, half, half_other)
    loss = loss[0, 0] / (2 * chips)
    return (loss, image_grad, text_grad, head_grad)


def solution(mesh):
    by_place = Mesh(mesh.devices.reshape(*GRID, 2), ("y", "x", "z", "core"))
    rows = P(("y", "x", "z", "core"), None)
    return jax.shard_map(
        per_device,
        mesh=by_place,
        in_specs=(rows, rows, P(), P(), P()),
        out_specs=(P(), rows, rows, P()),
        check_vma=False,
    )
```

```python
import functools
import math

import jax
import jax.numpy as jnp
from jax import lax
from jax.experimental import pallas as pl
from jax.experimental.pallas import tpu as pltpu
from jax.sharding import Mesh, PartitionSpec as P

D = 1152
E = 640
ROWS = 256
HALF = D // 2
LANES = 128
EPS = 1e-06
CHUNK = 64
FLAT = 3072
LONG = 10**11
GRID = (8, 4, 8)

BF = jnp.bfloat16
F32 = jnp.float32
VMEM = pl.BlockSpec(memory_space=pltpu.VMEM)
SMEM = pl.BlockSpec(memory_space=pltpu.SMEM)
PARAMS = pltpu.CompilerParams(vmem_limit_bytes=10 * 1024 * 1024)


def call(body, out_shape, n_smem, n_vmem, out_specs, scratch=(), flops=0, bytes_accessed=0):
    return pl.pallas_call(
        body,
        out_shape=out_shape,
        in_specs=[SMEM] * n_smem + [VMEM] * n_vmem,
        out_specs=out_specs,
        scratch_shapes=list(scratch),
        compiler_params=PARAMS,
        cost_estimate=pl.CostEstimate(flops=flops, bytes_accessed=bytes_accessed, transcendentals=0),
    )


def project_kernel(core_ref, own_ref, other_ref, weight_ref, zi_ref, zib_ref, inv_ref, xt_ref, all_ref):
    for part, ref in enumerate((own_ref, other_ref)):
        rows = pl.ds(part * ROWS, ROWS)
        all_ref[:, part * ROWS : (part + 1) * ROWS] = ref[...].T
        u = jnp.dot(ref[...], weight_ref[...], preferred_element_type=F32)
        inv = lax.rsqrt(jnp.sum(u * u, axis=1, keepdims=True) + EPS)
        zi = u * inv
        zi_ref[rows, :] = zi
        zib_ref[rows, :] = zi.astype(BF)
        inv_ref[rows, :] = jnp.broadcast_to(inv, (ROWS, LANES))
    xt_ref[...] = all_ref[pl.ds(pl.multiple_of(core_ref[0] * HALF, HALF), HALF), :]


def score_kernel(parts, has_dzi, scal_ref, zib_ref, *refs):
    text_refs, refs = refs[: len(parts)], refs[len(parts) :]
    dzi_in = None
    if has_dzi:
        dzi_in, *refs = refs
    dzi_ref, dzt_refs, (loss_ref, s_ref, c_ref) = refs[0], refs[1:-3], refs[-3:]
    scale = scal_ref[0]
    bias = scal_ref[1]
    loss = jnp.zeros((8, ROWS), F32)
    for q, (lo, hi, diag) in enumerate(parts):
        n = hi - lo
        text = text_refs[q][...].astype(F32)
        inv = lax.rsqrt(jnp.sum(text * text, axis=1, keepdims=True) + EPS)
        ztb = (text * inv).astype(BF)
        zib = zib_ref[lo:hi, :]
        s_ref[0:n, :] = lax.dot_general(zib, ztb, (((1,), (1,)), ((), ())), preferred_element_type=F32)
        for start in range(0, n, CHUNK):
            v = scale * s_ref[start : start + CHUNK, :] + bias
            paired = diag and start < ROWS
            if paired:
                row = lax.broadcasted_iota(jnp.int32, (CHUNK, ROWS), 0) + start
                col = lax.broadcasted_iota(jnp.int32, (CHUNK, ROWS), 1)
                own = row == col
                v = jnp.where(own, -v, v)
            e = jnp.exp(v)
            w = 1.0 + e
            r = 1.0 / w
            c = e * r
            if paired:
                c = jnp.where(own, -c, c)
            c_ref[start : start + CHUNK, :] = c.astype(BF)
            lost = (e - (w - 1.0)) * r
            loss = loss + jnp.sum(lost.reshape(CHUNK // 8, 8, ROWS), axis=0)
            k = CHUNK // 4
            prod = (w[0:k] * w[k : 2 * k]) * (w[2 * k : 3 * k] * w[3 * k :])
            loss = loss + jnp.sum(jnp.log(prod).reshape(k // 8, 8, ROWS), axis=0)
        coef = c_ref[0:n, :]
        dzi = scale * jnp.dot(coef, ztb, preferred_element_type=F32)
        if q:
            dzi_ref[lo:hi, :] += dzi
        elif has_dzi:
            dzi_ref[lo:hi, :] = dzi_in[lo:hi, :] + dzi
            if lo:
                dzi_ref[0:lo, :] = dzi_in[0:lo, :]
        else:
            dzi_ref[...] = dzi
        dzt = scale * lax.dot_general(coef, zib, (((0,), (0,)), ((), ())), preferred_element_type=F32)
        dzt_refs[q][...] = dzt.astype(dzt_refs[q].dtype)
    loss_ref[...] = loss


def score(parts, scal, zib, texts, dzi, dzt_dtype):
    args = (scal, zib, *texts) + (() if dzi is None else (dzi,))
    return call(
        functools.partial(score_kernel, parts, dzi is not None),
        (
            jax.ShapeDtypeStruct((2 * ROWS, E), F32),
            *(jax.ShapeDtypeStruct((ROWS, E), dzt_dtype) for _ in parts),
            jax.ShapeDtypeStruct((8, ROWS), F32),
        ),
        1,
        len(args) - 1,
        (VMEM,) * (len(parts) + 2),
        scratch=(pltpu.VMEM((2 * ROWS, ROWS), F32), pltpu.VMEM((2 * ROWS, ROWS), BF)),
        flops=sum(6 * (hi - lo) * ROWS * E for lo, hi, _ in parts),
        bytes_accessed=4 << 20,
    )(*args)


def head_kernel(dzi_ref, sent_ref, zi_ref, inv_ref, xt_ref, *refs):
    *loss_refs, du_ref, flat_ref, all_ref = refs
    for part in range(2):
        rows = pl.ds(part * ROWS, ROWS)
        swapped = pl.ds((1 - part) * ROWS, ROWS)
        dzi = dzi_ref[rows, :] + sent_ref[swapped, :]
        zi = zi_ref[rows, :]
        along = jnp.sum(zi * dzi, axis=1, keepdims=True)
        du = ((dzi - zi * along) * inv_ref[rows, 0:1]).astype(BF)
        all_ref[rows, :] = du
        if part == 0:
            du_ref[...] = du
    for slab in range(E // LANES):
        part = jnp.dot(xt_ref[...], all_ref[:, slab * LANES : (slab + 1) * LANES], preferred_element_type=F32)
        flat_ref[slab * HALF : (slab + 1) * HALF, :] = part.astype(BF)
    loss = jnp.sum(sum(ref[...] for ref in loss_refs))
    total = jnp.full((16, LANES), loss, F32)
    high = total.astype(BF).astype(F32)
    low = (total - high).astype(BF).astype(F32)
    row = lax.broadcasted_iota(jnp.int32, (16, LANES), 0)
    lane = lax.broadcasted_iota(jnp.int32, (16, LANES), 1)
    both = jnp.where(lane == 0, high, jnp.where(lane == 1, low, 0.0))
    base = (E // LANES) * HALF
    flat_ref[base : base + 16, :] = jnp.where(row == 0, both, 0.0).astype(BF)
    flat_ref[base + 16 :, :] = jnp.zeros((flat_ref.shape[0] - base - 16, LANES), BF)


def sum_kernel(pieces_ref, out_ref):
    n = out_ref.shape[0]
    for lo in range(0, n, n // 4):
        total = pieces_ref[lo : lo + n // 4, :].astype(F32)
        for first in range(n, pieces_ref.shape[0], n):
            total = total + pieces_ref[first + lo : first + lo + n // 4, :].astype(F32)
        out_ref[lo : lo + n // 4, :] = total.astype(BF)


def reduce_kernel(share, place_ref, pieces_ref, out_ref, sum_ref):
    group = sum_ref.shape[0]
    groups = pieces_ref.shape[0] // group
    total = jnp.zeros((group, LANES), F32)
    for g in range(groups):
        total = total + pieces_ref[g * group : (g + 1) * group, :].astype(F32)
    sum_ref[...] = total
    total = sum_ref[0:share, :]
    for k in range(1, group // share):
        total = total + sum_ref[k * share : (k + 1) * share, :]
    total = total * (1.0 / ROWS)
    loss_row = (E // LANES) * HALF
    row = lax.broadcasted_iota(jnp.int32, (share, LANES), 0)
    lane = lax.broadcasted_iota(jnp.int32, (share, LANES), 1)
    is_loss = (row == loss_row % share) & (place_ref[0] == loss_row // share)
    loss = jnp.sum(jnp.where(row == loss_row % share, total, 0.0), axis=(0, 1), keepdims=True)
    loss = jnp.broadcast_to(loss, (share, LANES))
    high = loss.astype(BF).astype(F32)
    terms = jnp.where(lane == 0, high, jnp.where(lane == 1, loss - high, 0.0))
    total = jnp.where(is_loss, terms, total)
    for k in range(group // share):
        sum_ref[k * share : (k + 1) * share, :] = total
    tile = sum_ref[...].astype(BF)
    for g in range(groups):
        out_ref[g * group : (g + 1) * group, :] = tile


def assemble_kernel(core_ref, own_ref, other_ref, head_ref, loss_ref):
    core = core_ref[0]
    for slab in range(E // LANES):
        for ref, half in ((own_ref, core), (other_ref, 1 - core)):
            rows = pl.ds(pl.multiple_of(half * HALF, HALF), HALF)
            head_ref[rows, slab * LANES : (slab + 1) * LANES] = ref[slab * HALF : (slab + 1) * HALF, :]
    base = (E // LANES) * HALF
    terms = own_ref[base : base + 16, :].astype(F32) + other_ref[base : base + 16, :].astype(F32)
    loss_ref[0, 0] = jnp.sum(terms)


def relay_kernel(far_same_ref, far_other_ref, near_same_ref, near_other_ref, same_ref, other_ref):
    same_ref[...] = (far_same_ref[...].astype(F32) + near_same_ref[...]).astype(BF)
    other_ref[...] = (far_other_ref[...].astype(F32) + near_other_ref[...]).astype(BF)


def join_kernel(own_ref, same_ref, out_ref):
    out_ref[...] = own_ref[...] + same_ref[...].astype(F32)


def text_kernel(joined_ref, other_ref, text_ref, out_ref):
    dzt = joined_ref[...] + other_ref[...].astype(F32)
    text = text_ref[...].astype(F32)
    inv = lax.rsqrt(jnp.sum(text * text, axis=1, keepdims=True) + EPS)
    zt = text * inv
    along = jnp.sum(zt * dzt, axis=1, keepdims=True)
    out_ref[...] = ((dzt - zt * along) * inv).astype(BF)


def per_device(image_feats, text_embeds, head_weight, logit_scale, logit_bias):
    axes = ("y", "x", "z", "core")
    ny, nx, nz = GRID
    chips = ny * nx * nz
    core = lax.axis_index("core")
    core_id = core.astype(jnp.int32).reshape(1)
    place = lax.axis_index(("x", "y", "z")).astype(jnp.int32).reshape(1)
    across = [(i, i ^ 1) for i in range(2 * chips)]
    onward = [(2 * k + b, 2 * ((k + 2 * b - 1) % chips) + b) for k in range(chips) for b in range(2)]
    beyond = [(2 * k + b, 2 * ((k + 4 * b - 2) % chips) + b) for k in range(chips) for b in range(2)]
    back = [(d, s) for s, d in onward]

    def crossing(step):
        return [(2 * k + b, 2 * ((k + step * (1 - 2 * b)) % chips) + 1 - b) for k in range(chips) for b in range(2)]

    scal = jnp.concatenate([logit_scale, logit_bias])

    near_same = lax.ppermute(text_embeds, axes, onward)
    x_other = lax.ppermute(image_feats, axes, across)
    near_other = lax.ppermute(text_embeds, axes, crossing(1))
    far_same = lax.ppermute(text_embeds, axes, beyond)
    far_other = lax.ppermute(text_embeds, axes, crossing(2))

    zi, zib, inv_u, x_half = call(
        project_kernel,
        (
            jax.ShapeDtypeStruct((2 * ROWS, E), F32),
            jax.ShapeDtypeStruct((2 * ROWS, E), BF),
            jax.ShapeDtypeStruct((2 * ROWS, LANES), F32),
            jax.ShapeDtypeStruct((HALF, 2 * ROWS), BF),
        ),
        1,
        3,
        (VMEM, VMEM, VMEM, VMEM),
        scratch=(pltpu.VMEM((D, 2 * ROWS), BF),),
        flops=2 * 2 * ROWS * D * E,
        bytes_accessed=5 << 20,
    )(core_id, image_feats, x_other, head_weight)

    both = 2 * ROWS
    whole = (0, both, False)
    dzi, dzt0, loss0 = score([(0, both, True)], scal, zib, [text_embeds], None, F32)
    dzi, far_other, loss2 = score([(ROWS, both, False)], scal, zib, [far_other], dzi, BF)
    dzi, far_same, loss1 = score([whole], scal, zib, [far_same], dzi, BF)
    dzi, near_other, loss4 = score([whole], scal, zib, [near_other], dzi, F32)
    dzi, near_same, loss3 = score([whole], scal, zib, [near_same], dzi, F32)
    dzi_sent = lax.ppermute(dzi, axes, across)

    du, flat = call(
        head_kernel,
        (
            jax.ShapeDtypeStruct((ROWS, E), BF),
            jax.ShapeDtypeStruct((FLAT, LANES), BF),
        ),
        0,
        10,
        (VMEM, VMEM),
        scratch=(pltpu.VMEM((2 * ROWS, E), BF),),
        flops=2 * 2 * ROWS * HALF * E,
        bytes_accessed=7 << 20,
    )(dzi, dzi_sent, zi, inv_u, x_half, loss0, loss1, loss2, loss3, loss4)

    part = FLAT // nx
    share = FLAT // chips
    along_x = lax.all_to_all(flat.reshape(nx, part, LANES), "x", 0, 0)
    summed = call(
        sum_kernel, jax.ShapeDtypeStruct((part, LANES), BF), 0, 1, VMEM, flops=FLAT * LANES, bytes_accessed=1 << 20
    )(along_x.reshape(FLAT, LANES))
    summed, far_same, far_other = lax.optimization_barrier((summed, far_same, far_other))
    far_same = lax.ppermute(far_same, axes, back)
    far_other = lax.ppermute(far_other, axes, back)
    pieces = lax.all_to_all(summed.reshape(ny * nz, share // 2, 2, LANES), ("y", "z"), 0, 0)
    same, other = call(
        relay_kernel,
        (jax.ShapeDtypeStruct((ROWS, E), BF), jax.ShapeDtypeStruct((ROWS, E), BF)),
        0,
        4,
        (VMEM, VMEM),
        flops=both * E,
        bytes_accessed=3 << 20,
    )(far_same, far_other, near_same, near_other)
    spread = call(
        functools.partial(reduce_kernel, share),
        jax.ShapeDtypeStruct((part, LANES), BF),
        1,
        1,
        VMEM,
        scratch=(pltpu.VMEM((math.lcm(share, 48), LANES), F32),),
        flops=part * LANES,
        bytes_accessed=1 << 20,
    )(place, pieces.reshape(part, LANES))
    home_same = lax.ppermute(same, axes, back)
    home_other = lax.ppermute(other, axes, [(s, d ^ 1) for s, d in back])
    mine = lax.all_to_all(spread.reshape(ny * nz, share // 2, 2, LANES), ("y", "z"), 0, 0).reshape(part, LANES)
    joined = call(
        join_kernel, jax.ShapeDtypeStruct((ROWS, E), F32), 0, 2, VMEM, flops=LONG, bytes_accessed=2 << 20
    )(dzt0, home_same)
    text_grad = call(
        text_kernel, jax.ShapeDtypeStruct((ROWS, E), BF), 0, 3, VMEM, flops=10 * ROWS * E, bytes_accessed=2 << 20
    )(joined, home_other, text_embeds)
    mine, du = lax.optimization_barrier((mine, du))
    image_grad = lax.dot_general(du, head_weight, (((1,), (1,)), ((), ())), preferred_element_type=F32).astype(BF)
    half = lax.all_to_all(jnp.broadcast_to(mine, (nx, part, LANES)), "x", 0, 0).reshape(FLAT, LANES)
    half, text_grad, image_grad = lax.optimization_barrier((half, text_grad, image_grad))
    half_other = lax.ppermute(half, axes, across)

    head_grad, loss = call(
        assemble_kernel,
        (jax.ShapeDtypeStruct((D, E), BF), jax.ShapeDtypeStruct((1, 1), F32)),
        1,
        2,
        (VMEM, SMEM),
        flops=1,
        bytes_accessed=3 << 20,
    )(core_id, half, half_other)
    loss = loss[0, 0] / (2 * chips)
    return (loss, image_grad, text_grad, head_grad)


def solution(mesh):
    by_place = Mesh(mesh.devices.reshape(*GRID, 2), ("y", "x", "z", "core"))
    rows = P(("y", "x", "z", "core"), None)
    return jax.shard_map(
        per_device,
        mesh=by_place,
        in_specs=(rows, rows, P(), P(), P()),
        out_specs=(P(), rows, rows, P()),
        check_vma=False,
    )
```

```python
import functools
import math

import jax
import jax.numpy as jnp
from jax import lax
from jax.experimental import pallas as pl
from jax.experimental.pallas import tpu as pltpu
from jax.sharding import Mesh, PartitionSpec as P

D = 1152
E = 640
ROWS = 256
HALF = D // 2
LANES = 128
EPS = 1e-06
CHUNK = 64
FLAT = 3072
LONG = 10**11
GRID = (8, 4, 8)

BF = jnp.bfloat16
F32 = jnp.float32
VMEM = pl.BlockSpec(memory_space=pltpu.VMEM)
SMEM = pl.BlockSpec(memory_space=pltpu.SMEM)
PARAMS = pltpu.CompilerParams(vmem_limit_bytes=10 * 1024 * 1024)


def call(body, out_shape, n_smem, n_vmem, out_specs, scratch=(), flops=0, bytes_accessed=0):
    return pl.pallas_call(
        body,
        out_shape=out_shape,
        in_specs=[SMEM] * n_smem + [VMEM] * n_vmem,
        out_specs=out_specs,
        scratch_shapes=list(scratch),
        compiler_params=PARAMS,
        cost_estimate=pl.CostEstimate(flops=flops, bytes_accessed=bytes_accessed, transcendentals=0),
    )


def project_kernel(core_ref, own_ref, other_ref, weight_ref, zi_ref, zib_ref, inv_ref, xt_ref, all_ref):
    for part, ref in enumerate((own_ref, other_ref)):
        rows = pl.ds(part * ROWS, ROWS)
        all_ref[:, part * ROWS : (part + 1) * ROWS] = ref[...].T
        u = jnp.dot(ref[...], weight_ref[...], preferred_element_type=F32)
        inv = lax.rsqrt(jnp.sum(u * u, axis=1, keepdims=True) + EPS)
        zi = u * inv
        zi_ref[rows, :] = zi
        zib_ref[rows, :] = zi.astype(BF)
        inv_ref[rows, :] = jnp.broadcast_to(inv, (ROWS, LANES))
    xt_ref[...] = all_ref[pl.ds(pl.multiple_of(core_ref[0] * HALF, HALF), HALF), :]


def score_kernel(parts, has_dzi, scal_ref, zib_ref, *refs):
    text_refs, refs = refs[: len(parts)], refs[len(parts) :]
    dzi_in = None
    if has_dzi:
        dzi_in, *refs = refs
    dzi_ref, dzt_refs, (loss_ref, s_ref, c_ref) = refs[0], refs[1:-3], refs[-3:]
    scale = scal_ref[0]
    bias = scal_ref[1]
    loss = jnp.zeros((8, ROWS), F32)
    for q, (lo, hi, diag) in enumerate(parts):
        n = hi - lo
        text = text_refs[q][...].astype(F32)
        inv = lax.rsqrt(jnp.sum(text * text, axis=1, keepdims=True) + EPS)
        ztb = (text * inv).astype(BF)
        zib = zib_ref[lo:hi, :]
        s_ref[0:n, :] = lax.dot_general(zib, ztb, (((1,), (1,)), ((), ())), preferred_element_type=F32)
        for start in range(0, n, CHUNK):
            v = scale * s_ref[start : start + CHUNK, :] + bias
            paired = diag and start < ROWS
            if paired:
                row = lax.broadcasted_iota(jnp.int32, (CHUNK, ROWS), 0) + start
                col = lax.broadcasted_iota(jnp.int32, (CHUNK, ROWS), 1)
                own = row == col
                v = jnp.where(own, -v, v)
            e = jnp.exp(v)
            w = 1.0 + e
            r = 1.0 / w
            c = e * r
            if paired:
                c = jnp.where(own, -c, c)
            c_ref[start : start + CHUNK, :] = c.astype(BF)
            lost = (e - (w - 1.0)) * r
            loss = loss + jnp.sum(lost.reshape(CHUNK // 8, 8, ROWS), axis=0)
            k = CHUNK // 4
            prod = (w[0:k] * w[k : 2 * k]) * (w[2 * k : 3 * k] * w[3 * k :])
            loss = loss + jnp.sum(jnp.log(prod).reshape(k // 8, 8, ROWS), axis=0)
        coef = c_ref[0:n, :]
        dzi = scale * jnp.dot(coef, ztb, preferred_element_type=F32)
        if q:
            dzi_ref[lo:hi, :] += dzi
        elif has_dzi:
            dzi_ref[lo:hi, :] = dzi_in[lo:hi, :] + dzi
            if lo:
                dzi_ref[0:lo, :] = dzi_in[0:lo, :]
        else:
            dzi_ref[...] = dzi
        dzt = scale * lax.dot_general(coef, zib, (((0,), (0,)), ((), ())), preferred_element_type=F32)
        dzt_refs[q][...] = dzt.astype(dzt_refs[q].dtype)
    loss_ref[...] = loss


def score(parts, scal, zib, texts, dzi, dzt_dtype):
    args = (scal, zib, *texts) + (() if dzi is None else (dzi,))
    return call(
        functools.partial(score_kernel, parts, dzi is not None),
        (
            jax.ShapeDtypeStruct((2 * ROWS, E), F32),
            *(jax.ShapeDtypeStruct((ROWS, E), dzt_dtype) for _ in parts),
            jax.ShapeDtypeStruct((8, ROWS), F32),
        ),
        1,
        len(args) - 1,
        (VMEM,) * (len(parts) + 2),
        scratch=(pltpu.VMEM((2 * ROWS, ROWS), F32), pltpu.VMEM((2 * ROWS, ROWS), BF)),
        flops=sum(6 * (hi - lo) * ROWS * E for lo, hi, _ in parts),
        bytes_accessed=4 << 20,
    )(*args)


def head_kernel(dzi_ref, sent_ref, zi_ref, inv_ref, xt_ref, *refs):
    *loss_refs, du_ref, flat_ref, all_ref = refs
    for part in range(2):
        rows = pl.ds(part * ROWS, ROWS)
        swapped = pl.ds((1 - part) * ROWS, ROWS)
        dzi = dzi_ref[rows, :] + sent_ref[swapped, :]
        zi = zi_ref[rows, :]
        along = jnp.sum(zi * dzi, axis=1, keepdims=True)
        du = ((dzi - zi * along) * inv_ref[rows, 0:1]).astype(BF)
        all_ref[rows, :] = du
        if part == 0:
            du_ref[...] = du
    for slab in range(E // LANES):
        part = jnp.dot(xt_ref[...], all_ref[:, slab * LANES : (slab + 1) * LANES], preferred_element_type=F32)
        flat_ref[slab * HALF : (slab + 1) * HALF, :] = part.astype(BF)
    loss = jnp.sum(sum(ref[...] for ref in loss_refs))
    total = jnp.full((16, LANES), loss, F32)
    high = total.astype(BF).astype(F32)
    low = (total - high).astype(BF).astype(F32)
    row = lax.broadcasted_iota(jnp.int32, (16, LANES), 0)
    lane = lax.broadcasted_iota(jnp.int32, (16, LANES), 1)
    both = jnp.where(lane == 0, high, jnp.where(lane == 1, low, 0.0))
    base = (E // LANES) * HALF
    flat_ref[base : base + 16, :] = jnp.where(row == 0, both, 0.0).astype(BF)
    flat_ref[base + 16 :, :] = jnp.zeros((flat_ref.shape[0] - base - 16, LANES), BF)


def sum_kernel(pieces_ref, out_ref):
    n = out_ref.shape[0]
    for lo in range(0, n, n // 4):
        total = pieces_ref[lo : lo + n // 4, :].astype(F32)
        for first in range(n, pieces_ref.shape[0], n):
            total = total + pieces_ref[first + lo : first + lo + n // 4, :].astype(F32)
        out_ref[lo : lo + n // 4, :] = total.astype(BF)


def reduce_kernel(share, place_ref, pieces_ref, out_ref, sum_ref):
    group = sum_ref.shape[0]
    groups = pieces_ref.shape[0] // group
    total = jnp.zeros((group, LANES), F32)
    for g in range(groups):
        total = total + pieces_ref[g * group : (g + 1) * group, :].astype(F32)
    sum_ref[...] = total
    total = sum_ref[0:share, :]
    for k in range(1, group // share):
        total = total + sum_ref[k * share : (k + 1) * share, :]
    total = total * (1.0 / ROWS)
    loss_row = (E // LANES) * HALF
    row = lax.broadcasted_iota(jnp.int32, (share, LANES), 0)
    lane = lax.broadcasted_iota(jnp.int32, (share, LANES), 1)
    is_loss = (row == loss_row % share) & (place_ref[0] == loss_row // share)
    loss = jnp.sum(jnp.where(row == loss_row % share, total, 0.0), axis=(0, 1), keepdims=True)
    loss = jnp.broadcast_to(loss, (share, LANES))
    high = loss.astype(BF).astype(F32)
    terms = jnp.where(lane == 0, high, jnp.where(lane == 1, loss - high, 0.0))
    total = jnp.where(is_loss, terms, total)
    for k in range(group // share):
        sum_ref[k * share : (k + 1) * share, :] = total
    tile = sum_ref[...].astype(BF)
    for g in range(groups):
        out_ref[g * group : (g + 1) * group, :] = tile


def assemble_kernel(core_ref, own_ref, other_ref, head_ref, loss_ref):
    core = core_ref[0]
    for slab in range(E // LANES):
        for ref, half in ((own_ref, core), (other_ref, 1 - core)):
            rows = pl.ds(pl.multiple_of(half * HALF, HALF), HALF)
            head_ref[rows, slab * LANES : (slab + 1) * LANES] = ref[slab * HALF : (slab + 1) * HALF, :]
    base = (E // LANES) * HALF
    terms = own_ref[base : base + 16, :].astype(F32) + other_ref[base : base + 16, :].astype(F32)
    loss_ref[0, 0] = jnp.sum(terms)


def relay_kernel(far_same_ref, far_other_ref, near_same_ref, near_other_ref, same_ref, other_ref):
    same_ref[...] = (far_same_ref[...].astype(F32) + near_same_ref[...]).astype(BF)
    other_ref[...] = (far_other_ref[...].astype(F32) + near_other_ref[...]).astype(BF)


def join_kernel(own_ref, same_ref, out_ref):
    out_ref[...] = own_ref[...] + same_ref[...].astype(F32)


def text_kernel(joined_ref, other_ref, text_ref, out_ref):
    dzt = joined_ref[...] + other_ref[...].astype(F32)
    text = text_ref[...].astype(F32)
    inv = lax.rsqrt(jnp.sum(text * text, axis=1, keepdims=True) + EPS)
    zt = text * inv
    along = jnp.sum(zt * dzt, axis=1, keepdims=True)
    out_ref[...] = ((dzt - zt * along) * inv).astype(BF)


def per_device(image_feats, text_embeds, head_weight, logit_scale, logit_bias):
    axes = ("y", "x", "z", "core")
    ny, nx, nz = GRID
    chips = ny * nx * nz
    core = lax.axis_index("core")
    core_id = core.astype(jnp.int32).reshape(1)
    place = lax.axis_index(("x", "y", "z")).astype(jnp.int32).reshape(1)
    across = [(i, i ^ 1) for i in range(2 * chips)]
    onward = [(2 * k + b, 2 * ((k + 2 * b - 1) % chips) + b) for k in range(chips) for b in range(2)]
    beyond = [(2 * k + b, 2 * ((k + 4 * b - 2) % chips) + b) for k in range(chips) for b in range(2)]
    back = [(d, s) for s, d in onward]

    def crossing(step):
        return [(2 * k + b, 2 * ((k + step * (1 - 2 * b)) % chips) + 1 - b) for k in range(chips) for b in range(2)]

    scal = jnp.concatenate([logit_scale, logit_bias])

    near_same = lax.ppermute(text_embeds, axes, onward)
    x_other = lax.ppermute(image_feats, axes, across)
    near_other = lax.ppermute(text_embeds, axes, crossing(1))
    far_same = lax.ppermute(text_embeds, axes, beyond)
    far_other = lax.ppermute(text_embeds, axes, crossing(2))

    zi, zib, inv_u, x_half = call(
        project_kernel,
        (
            jax.ShapeDtypeStruct((2 * ROWS, E), F32),
            jax.ShapeDtypeStruct((2 * ROWS, E), BF),
            jax.ShapeDtypeStruct((2 * ROWS, LANES), F32),
            jax.ShapeDtypeStruct((HALF, 2 * ROWS), BF),
        ),
        1,
        3,
        (VMEM, VMEM, VMEM, VMEM),
        scratch=(pltpu.VMEM((D, 2 * ROWS), BF),),
        flops=2 * 2 * ROWS * D * E,
        bytes_accessed=5 << 20,
    )(core_id, image_feats, x_other, head_weight)

    both = 2 * ROWS
    whole = (0, both, False)
    dzi, dzt0, loss0 = score([(0, both, True)], scal, zib, [text_embeds], None, F32)
    dzi, far_same, far_other, loss1 = score([whole, (ROWS, both, False)], scal, zib, [far_same, far_other], dzi, BF)
    dzi, near_other, loss2 = score([whole], scal, zib, [near_other], dzi, F32)
    dzi, near_same, loss3 = score([whole], scal, zib, [near_same], dzi, F32)
    dzi_sent = lax.ppermute(dzi, axes, across)

    du, flat = call(
        head_kernel,
        (
            jax.ShapeDtypeStruct((ROWS, E), BF),
            jax.ShapeDtypeStruct((FLAT, LANES), BF),
        ),
        0,
        9,
        (VMEM, VMEM),
        scratch=(pltpu.VMEM((2 * ROWS, E), BF),),
        flops=2 * 2 * ROWS * HALF * E,
        bytes_accessed=7 << 20,
    )(dzi, dzi_sent, zi, inv_u, x_half, loss0, loss1, loss2, loss3)

    part = FLAT // nx
    share = FLAT // chips
    along_x = lax.all_to_all(flat.reshape(nx, part, LANES), "x", 0, 0)
    summed = call(
        sum_kernel, jax.ShapeDtypeStruct((part, LANES), BF), 0, 1, VMEM, flops=FLAT * LANES, bytes_accessed=1 << 20
    )(along_x.reshape(FLAT, LANES))
    summed, far_same, far_other = lax.optimization_barrier((summed, far_same, far_other))
    far_same = lax.ppermute(far_same, axes, back)
    far_other = lax.ppermute(far_other, axes, back)
    pieces = lax.all_to_all(summed.reshape(ny * nz, share // 2, 2, LANES), ("y", "z"), 0, 0)
    same, other = call(
        relay_kernel,
        (jax.ShapeDtypeStruct((ROWS, E), BF), jax.ShapeDtypeStruct((ROWS, E), BF)),
        0,
        4,
        (VMEM, VMEM),
        flops=both * E,
        bytes_accessed=3 << 20,
    )(far_same, far_other, near_same, near_other)
    spread = call(
        functools.partial(reduce_kernel, share),
        jax.ShapeDtypeStruct((part, LANES), BF),
        1,
        1,
        VMEM,
        scratch=(pltpu.VMEM((math.lcm(share, 48), LANES), F32),),
        flops=part * LANES,
        bytes_accessed=1 << 20,
    )(place, pieces.reshape(part, LANES))
    home_same = lax.ppermute(same, axes, back)
    home_other = lax.ppermute(other, axes, [(s, d ^ 1) for s, d in back])
    mine = lax.all_to_all(spread.reshape(ny * nz, share // 2, 2, LANES), ("y", "z"), 0, 0).reshape(part, LANES)
    joined = call(
        join_kernel, jax.ShapeDtypeStruct((ROWS, E), F32), 0, 2, VMEM, flops=LONG, bytes_accessed=2 << 20
    )(dzt0, home_same)
    text_grad = call(
        text_kernel, jax.ShapeDtypeStruct((ROWS, E), BF), 0, 3, VMEM, flops=10 * ROWS * E, bytes_accessed=2 << 20
    )(joined, home_other, text_embeds)
    mine, du = lax.optimization_barrier((mine, du))
    image_grad = lax.dot_general(du, head_weight, (((1,), (1,)), ((), ())), preferred_element_type=F32).astype(BF)
    half = lax.all_to_all(jnp.broadcast_to(mine, (nx, part, LANES)), "x", 0, 0).reshape(FLAT, LANES)
    half, text_grad, image_grad = lax.optimization_barrier((half, text_grad, image_grad))
    half_other = lax.ppermute(half, axes, across)

    head_grad, loss = call(
        assemble_kernel,
        (jax.ShapeDtypeStruct((D, E), BF), jax.ShapeDtypeStruct((1, 1), F32)),
        1,
        2,
        (VMEM, SMEM),
        flops=1,
        bytes_accessed=3 << 20,
    )(core_id, half, half_other)
    loss = loss[0, 0] / (2 * chips)
    return (loss, image_grad, text_grad, head_grad)


def solution(mesh):
    by_place = Mesh(mesh.devices.reshape(*GRID, 2), ("y", "x", "z", "core"))
    rows = P(("y", "x", "z", "core"), None)
    return jax.shard_map(
        per_device,
        mesh=by_place,
        in_specs=(rows, rows, P(), P(), P()),
        out_specs=(P(), rows, rows, P()),
        check_vma=False,
    )
```

```python
import functools
import math

import jax
import jax.numpy as jnp
from jax import lax
from jax.experimental import pallas as pl
from jax.experimental.pallas import tpu as pltpu
from jax.sharding import Mesh, PartitionSpec as P

D = 1152
E = 640
ROWS = 256
HALF = D // 2
LANES = 128
EPS = 1e-06
CHUNK = 64
FLAT = 3072
LONG = 10**11
GRID = (8, 4, 8)

BF = jnp.bfloat16
F32 = jnp.float32
VMEM = pl.BlockSpec(memory_space=pltpu.VMEM)
SMEM = pl.BlockSpec(memory_space=pltpu.SMEM)
PARAMS = pltpu.CompilerParams(vmem_limit_bytes=10 * 1024 * 1024)


def call(body, out_shape, n_smem, n_vmem, out_specs, scratch=(), flops=0, bytes_accessed=0):
    return pl.pallas_call(
        body,
        out_shape=out_shape,
        in_specs=[SMEM] * n_smem + [VMEM] * n_vmem,
        out_specs=out_specs,
        scratch_shapes=list(scratch),
        compiler_params=PARAMS,
        cost_estimate=pl.CostEstimate(flops=flops, bytes_accessed=bytes_accessed, transcendentals=0),
    )


def project_kernel(core_ref, own_ref, other_ref, weight_ref, zi_ref, zib_ref, inv_ref, xt_ref, all_ref):
    for part, ref in enumerate((own_ref, other_ref)):
        rows = pl.ds(part * ROWS, ROWS)
        all_ref[:, part * ROWS : (part + 1) * ROWS] = ref[...].T
        u = jnp.dot(ref[...], weight_ref[...], preferred_element_type=F32)
        inv = lax.rsqrt(jnp.sum(u * u, axis=1, keepdims=True) + EPS)
        zi = u * inv
        zi_ref[rows, :] = zi
        zib_ref[rows, :] = zi.astype(BF)
        inv_ref[rows, :] = jnp.broadcast_to(inv, (ROWS, LANES))
    xt_ref[...] = all_ref[pl.ds(pl.multiple_of(core_ref[0] * HALF, HALF), HALF), :]


def score_kernel(parts, has_dzi, last, scal_ref, zib_ref, *refs):
    text_refs, refs = refs[: len(parts)], refs[len(parts) :]
    dzi_in = None
    if has_dzi:
        dzi_in, *refs = refs
    if last:
        sent_ref, *refs = refs
    dzi_ref, dzt_refs, (loss_ref, s_ref, c_ref) = refs[0], refs[1:-3], refs[-3:]
    scale = scal_ref[0]
    bias = scal_ref[1]
    loss = jnp.zeros((8, ROWS), F32)
    for q, (lo, hi, diag) in enumerate(parts):
        n = hi - lo
        text = text_refs[q][...].astype(F32)
        inv = lax.rsqrt(jnp.sum(text * text, axis=1, keepdims=True) + EPS)
        ztb = (text * inv).astype(BF)
        zib = zib_ref[lo:hi, :]
        s_ref[0:n, :] = lax.dot_general(zib, ztb, (((1,), (1,)), ((), ())), preferred_element_type=F32)
        for start in range(0, n, CHUNK):
            v = scale * s_ref[start : start + CHUNK, :] + bias
            paired = diag and start < ROWS
            if paired:
                row = lax.broadcasted_iota(jnp.int32, (CHUNK, ROWS), 0) + start
                col = lax.broadcasted_iota(jnp.int32, (CHUNK, ROWS), 1)
                own = row == col
                v = jnp.where(own, -v, v)
            e = jnp.exp(v)
            w = 1.0 + e
            r = 1.0 / w
            c = e * r
            if paired:
                c = jnp.where(own, -c, c)
            c_ref[start : start + CHUNK, :] = c.astype(BF)
            lost = (e - (w - 1.0)) * r
            loss = loss + jnp.sum(lost.reshape(CHUNK // 8, 8, ROWS), axis=0)
            k = CHUNK // 4
            prod = (w[0:k] * w[k : 2 * k]) * (w[2 * k : 3 * k] * w[3 * k :])
            loss = loss + jnp.sum(jnp.log(prod).reshape(k // 8, 8, ROWS), axis=0)
        coef = c_ref[0:n, :]
        dzi = scale * jnp.dot(coef, ztb, preferred_element_type=F32)
        if q:
            dzi_ref[lo:hi, :] += dzi
        elif has_dzi:
            dzi_ref[lo:hi, :] = dzi_in[lo:hi, :] + dzi
            if lo:
                dzi_ref[0:lo, :] = dzi_in[0:lo, :]
        else:
            dzi_ref[...] = dzi
        dzt = scale * lax.dot_general(coef, zib, (((0,), (0,)), ((), ())), preferred_element_type=F32)
        dzt_refs[q][...] = dzt.astype(dzt_refs[q].dtype)
    loss_ref[...] = loss
    if last:
        sent_ref[...] = dzi_ref[...].astype(BF)


def score(parts, scal, zib, texts, dzi, dzt_dtype, last=False):
    args = (scal, zib, *texts) + (() if dzi is None else (dzi,))
    return call(
        functools.partial(score_kernel, parts, dzi is not None, last),
        (
            *([jax.ShapeDtypeStruct((2 * ROWS, E), BF)] if last else []),
            jax.ShapeDtypeStruct((2 * ROWS, E), F32),
            *(jax.ShapeDtypeStruct((ROWS, E), dzt_dtype) for _ in parts),
            jax.ShapeDtypeStruct((8, ROWS), F32),
        ),
        1,
        len(args) - 1,
        (VMEM,) * (len(parts) + 2 + last),
        scratch=(pltpu.VMEM((2 * ROWS, ROWS), F32), pltpu.VMEM((2 * ROWS, ROWS), BF)),
        flops=sum(6 * (hi - lo) * ROWS * E for lo, hi, _ in parts),
        bytes_accessed=4 << 20,
    )(*args)


def head_kernel(dzi_ref, sent_ref, zi_ref, inv_ref, xt_ref, *refs):
    *loss_refs, du_ref, flat_ref, all_ref = refs
    for part in range(2):
        rows = pl.ds(part * ROWS, ROWS)
        swapped = pl.ds((1 - part) * ROWS, ROWS)
        dzi = dzi_ref[rows, :] + sent_ref[swapped, :].astype(F32)
        zi = zi_ref[rows, :]
        along = jnp.sum(zi * dzi, axis=1, keepdims=True)
        du = ((dzi - zi * along) * inv_ref[rows, 0:1]).astype(BF)
        all_ref[rows, :] = du
        if part == 0:
            du_ref[...] = du
    for slab in range(E // LANES):
        part = jnp.dot(xt_ref[...], all_ref[:, slab * LANES : (slab + 1) * LANES], preferred_element_type=F32)
        flat_ref[slab * HALF : (slab + 1) * HALF, :] = part.astype(BF)
    loss = jnp.sum(sum(ref[...] for ref in loss_refs))
    total = jnp.full((16, LANES), loss, F32)
    high = total.astype(BF).astype(F32)
    low = (total - high).astype(BF).astype(F32)
    row = lax.broadcasted_iota(jnp.int32, (16, LANES), 0)
    lane = lax.broadcasted_iota(jnp.int32, (16, LANES), 1)
    both = jnp.where(lane == 0, high, jnp.where(lane == 1, low, 0.0))
    base = (E // LANES) * HALF
    flat_ref[base : base + 16, :] = jnp.where(row == 0, both, 0.0).astype(BF)
    flat_ref[base + 16 :, :] = jnp.zeros((flat_ref.shape[0] - base - 16, LANES), BF)


def sum_kernel(pieces_ref, out_ref):
    n = out_ref.shape[0]
    for lo in range(0, n, n // 4):
        total = pieces_ref[lo : lo + n // 4, :].astype(F32)
        for first in range(n, pieces_ref.shape[0], n):
            total = total + pieces_ref[first + lo : first + lo + n // 4, :].astype(F32)
        out_ref[lo : lo + n // 4, :] = total.astype(BF)


def reduce_kernel(share, place_ref, pieces_ref, out_ref, sum_ref):
    group = sum_ref.shape[0]
    groups = pieces_ref.shape[0] // group
    total = jnp.zeros((group, LANES), F32)
    for g in range(groups):
        total = total + pieces_ref[g * group : (g + 1) * group, :].astype(F32)
    sum_ref[...] = total
    total = sum_ref[0:share, :]
    for k in range(1, group // share):
        total = total + sum_ref[k * share : (k + 1) * share, :]
    total = total * (1.0 / ROWS)
    loss_row = (E // LANES) * HALF
    row = lax.broadcasted_iota(jnp.int32, (share, LANES), 0)
    lane = lax.broadcasted_iota(jnp.int32, (share, LANES), 1)
    is_loss = (row == loss_row % share) & (place_ref[0] == loss_row // share)
    loss = jnp.sum(jnp.where(row == loss_row % share, total, 0.0), axis=(0, 1), keepdims=True)
    loss = jnp.broadcast_to(loss, (share, LANES))
    high = loss.astype(BF).astype(F32)
    terms = jnp.where(lane == 0, high, jnp.where(lane == 1, loss - high, 0.0))
    total = jnp.where(is_loss, terms, total)
    for k in range(group // share):
        sum_ref[k * share : (k + 1) * share, :] = total
    tile = sum_ref[...].astype(BF)
    for g in range(groups):
        out_ref[g * group : (g + 1) * group, :] = tile


def assemble_kernel(core_ref, own_ref, other_ref, head_ref, loss_ref):
    core = core_ref[0]
    for slab in range(E // LANES):
        for ref, half in ((own_ref, core), (other_ref, 1 - core)):
            rows = pl.ds(pl.multiple_of(half * HALF, HALF), HALF)
            head_ref[rows, slab * LANES : (slab + 1) * LANES] = ref[slab * HALF : (slab + 1) * HALF, :]
    base = (E // LANES) * HALF
    terms = own_ref[base : base + 16, :].astype(F32) + other_ref[base : base + 16, :].astype(F32)
    loss_ref[0, 0] = jnp.sum(terms)


def relay_kernel(far_same_ref, far_other_ref, near_same_ref, near_other_ref, same_ref, other_ref):
    same_ref[...] = (far_same_ref[...].astype(F32) + near_same_ref[...]).astype(BF)
    other_ref[...] = (far_other_ref[...].astype(F32) + near_other_ref[...]).astype(BF)


def join_kernel(own_ref, same_ref, out_ref):
    out_ref[...] = own_ref[...] + same_ref[...].astype(F32)


def text_kernel(joined_ref, other_ref, text_ref, out_ref):
    dzt = joined_ref[...] + other_ref[...].astype(F32)
    text = text_ref[...].astype(F32)
    inv = lax.rsqrt(jnp.sum(text * text, axis=1, keepdims=True) + EPS)
    zt = text * inv
    along = jnp.sum(zt * dzt, axis=1, keepdims=True)
    out_ref[...] = ((dzt - zt * along) * inv).astype(BF)


def per_device(image_feats, text_embeds, head_weight, logit_scale, logit_bias):
    axes = ("y", "x", "z", "core")
    ny, nx, nz = GRID
    chips = ny * nx * nz
    core = lax.axis_index("core")
    core_id = core.astype(jnp.int32).reshape(1)
    place = lax.axis_index(("x", "y", "z")).astype(jnp.int32).reshape(1)
    across = [(i, i ^ 1) for i in range(2 * chips)]
    onward = [(2 * k + b, 2 * ((k + 2 * b - 1) % chips) + b) for k in range(chips) for b in range(2)]
    beyond = [(2 * k + b, 2 * ((k + 4 * b - 2) % chips) + b) for k in range(chips) for b in range(2)]
    back = [(d, s) for s, d in onward]

    def crossing(step):
        return [(2 * k + b, 2 * ((k + step * (1 - 2 * b)) % chips) + 1 - b) for k in range(chips) for b in range(2)]

    scal = jnp.concatenate([logit_scale, logit_bias])

    near_same = lax.ppermute(text_embeds, axes, onward)
    x_other = lax.ppermute(image_feats, axes, across)
    near_other = lax.ppermute(text_embeds, axes, crossing(1))
    far_same = lax.ppermute(text_embeds, axes, beyond)
    far_other = lax.ppermute(text_embeds, axes, crossing(2))

    zi, zib, inv_u, x_half = call(
        project_kernel,
        (
            jax.ShapeDtypeStruct((2 * ROWS, E), F32),
            jax.ShapeDtypeStruct((2 * ROWS, E), BF),
            jax.ShapeDtypeStruct((2 * ROWS, LANES), F32),
            jax.ShapeDtypeStruct((HALF, 2 * ROWS), BF),
        ),
        1,
        3,
        (VMEM, VMEM, VMEM, VMEM),
        scratch=(pltpu.VMEM((D, 2 * ROWS), BF),),
        flops=2 * 2 * ROWS * D * E,
        bytes_accessed=5 << 20,
    )(core_id, image_feats, x_other, head_weight)

    both = 2 * ROWS
    whole = (0, both, False)
    dzi, dzt0, loss0 = score([(0, both, True)], scal, zib, [text_embeds], None, F32)
    dzi, far_other, loss2 = score([(ROWS, both, False)], scal, zib, [far_other], dzi, BF)
    dzi, far_same, loss1 = score([whole], scal, zib, [far_same], dzi, BF)
    dzi, near_other, loss4 = score([whole], scal, zib, [near_other], dzi, F32)
    rounded, dzi, near_same, loss3 = score([whole], scal, zib, [near_same], dzi, F32, last=True)
    dzi_sent = lax.ppermute(rounded, axes, across)

    du, flat = call(
        head_kernel,
        (
            jax.ShapeDtypeStruct((ROWS, E), BF),
            jax.ShapeDtypeStruct((FLAT, LANES), BF),
        ),
        0,
        10,
        (VMEM, VMEM),
        scratch=(pltpu.VMEM((2 * ROWS, E), BF),),
        flops=2 * 2 * ROWS * HALF * E,
        bytes_accessed=7 << 20,
    )(dzi, dzi_sent, zi, inv_u, x_half, loss0, loss1, loss2, loss3, loss4)

    part = FLAT // nx
    share = FLAT // chips
    along_x = lax.all_to_all(flat.reshape(nx, part, LANES), "x", 0, 0)
    summed = call(
        sum_kernel, jax.ShapeDtypeStruct((part, LANES), BF), 0, 1, VMEM, flops=FLAT * LANES, bytes_accessed=1 << 20
    )(along_x.reshape(FLAT, LANES))
    summed, far_same, far_other = lax.optimization_barrier((summed, far_same, far_other))
    far_same = lax.ppermute(far_same, axes, back)
    far_other = lax.ppermute(far_other, axes, back)
    pieces = lax.all_to_all(summed.reshape(ny * nz, share // 2, 2, LANES), ("y", "z"), 0, 0)
    same, other = call(
        relay_kernel,
        (jax.ShapeDtypeStruct((ROWS, E), BF), jax.ShapeDtypeStruct((ROWS, E), BF)),
        0,
        4,
        (VMEM, VMEM),
        flops=both * E,
        bytes_accessed=3 << 20,
    )(far_same, far_other, near_same, near_other)
    spread = call(
        functools.partial(reduce_kernel, share),
        jax.ShapeDtypeStruct((part, LANES), BF),
        1,
        1,
        VMEM,
        scratch=(pltpu.VMEM((math.lcm(share, 48), LANES), F32),),
        flops=part * LANES,
        bytes_accessed=1 << 20,
    )(place, pieces.reshape(part, LANES))
    home_same = lax.ppermute(same, axes, back)
    home_other = lax.ppermute(other, axes, [(s, d ^ 1) for s, d in back])
    mine = lax.all_to_all(spread.reshape(ny * nz, share // 2, 2, LANES), ("y", "z"), 0, 0).reshape(part, LANES)
    joined = call(
        join_kernel, jax.ShapeDtypeStruct((ROWS, E), F32), 0, 2, VMEM, flops=LONG, bytes_accessed=2 << 20
    )(dzt0, home_same)
    text_grad = call(
        text_kernel, jax.ShapeDtypeStruct((ROWS, E), BF), 0, 3, VMEM, flops=10 * ROWS * E, bytes_accessed=2 << 20
    )(joined, home_other, text_embeds)
    mine, du = lax.optimization_barrier((mine, du))
    image_grad = lax.dot_general(du, head_weight, (((1,), (1,)), ((), ())), preferred_element_type=F32).astype(BF)
    half = lax.all_to_all(jnp.broadcast_to(mine, (nx, part, LANES)), "x", 0, 0).reshape(FLAT, LANES)
    half, text_grad, image_grad = lax.optimization_barrier((half, text_grad, image_grad))
    half_other = lax.ppermute(half, axes, across)

    head_grad, loss = call(
        assemble_kernel,
        (jax.ShapeDtypeStruct((D, E), BF), jax.ShapeDtypeStruct((1, 1), F32)),
        1,
        2,
        (VMEM, SMEM),
        flops=1,
        bytes_accessed=3 << 20,
    )(core_id, half, half_other)
    loss = loss[0, 0] / (2 * chips)
    return (loss, image_grad, text_grad, head_grad)


def solution(mesh):
    by_place = Mesh(mesh.devices.reshape(*GRID, 2), ("y", "x", "z", "core"))
    rows = P(("y", "x", "z", "core"), None)
    return jax.shard_map(
        per_device,
        mesh=by_place,
        in_specs=(rows, rows, P(), P(), P()),
        out_specs=(P(), rows, rows, P()),
        check_vma=False,
    )
```
